256 devices in a mesh: grp: 8 (over y, core), seq: 32 (over z, x).
Axes of the slice: x: 4, y: 4, z: 8, core: 2. Of those that a mesh axis runs over, the one named last changes fastest.
Arguments:
- inputs: bfloat16 [8, 32768, 512], P('grp', 'seq'), may hold values from -6 to 6
- offsets: int32 [8, 32768], P('grp', 'seq'), may hold values from 0 to 8191, as said below
- conv_weight: bfloat16 [2, 512, 1024], replicated, may hold values from -0.1875 to 0.1875
- res_weight: bfloat16 [512, 512], replicated, may hold values from -0.25 to 0.25
- cotangent: bfloat16 [8, 32768, 512], P('grp', 'seq'), may hold values from -6 to 6
Outputs:
- output: bfloat16 [8, 32768, 512], P('grp', 'seq')
- d_inputs: bfloat16 [8, 32768, 512], P('grp', 'seq')
- d_conv: float32 [2, 512, 1024], P(None, None, 'seq')
- d_res: float32 [512, 512], P(None, 'seq')
The draws below stay inside these ranges and needn't reach their ends.
Inputs may be any that keep to these rules, and one draw needn't show every extreme that they name: In each stream the offsets are 0 where a note begins (always at position 0) and elsewhere one more than the entry before; a note spans at most 8192 samples.
All inputs are finite; a program needn't handle non-finite values.
Results may differ from the reference program's by a relative error of at most 0.0029.
Values may be sent and summed in bfloat16 or wider, within the bound.
No kernel may reach another device: no remote copies, remote signals or barrier semaphores. Data moves between devices by JAX's collectives and lax.ppermute only.
A program may use at most 64 MiB of HBM per device.

```python
import math
import jax
import jax.numpy as jnp
from jax import lax

RESIDUAL_WIDTH = 512
GATES = 1024
DILATION_GAP = 4096
DEVICE_SAMPLES = 1024
LENGTH = 32768
STREAMS = 8
N_GRP = 8
N_SEQ = 32


def draw_offsets(key, part):
    key = jax.random.fold_in(key, 11)
    reach_length = 2 * DILATION_GAP
    note_starts = jax.random.randint(key, (N_GRP, DEVICE_SAMPLES * N_SEQ), 0, 4 * DILATION_GAP) == 0
    position = lax.broadcasted_iota(jnp.int32, (N_GRP, DEVICE_SAMPLES * N_SEQ), 1)
    stream_idx = lax.broadcasted_iota(jnp.int32, (N_GRP, DEVICE_SAMPLES * N_SEQ), 0)
    quiet = (stream_idx == 0) & (position < reach_length)
    note_starts = note_starts & jnp.logical_not(quiet)
    forced = ((position + stream_idx * (DEVICE_SAMPLES // 2)) % reach_length == 0) | (position == 0)
    starts = jnp.where(note_starts | forced, position, jnp.zeros_like(position))
    latest = lax.cummax(starts, axis=1)
    return (position - latest).astype(jnp.int32)


def strengthened(array, rng, source, target, parts, factor):
    owner, partner = [(jnp.arange(array.shape[axis_at]) // (array.shape[axis_at] // parts)).reshape([-1 if axis == axis_at else 1 for axis in range(array.ndim)]) for axis_at in (source, target)]
    chosen = jax.random.permutation(rng, parts)[partner]
    strong = (owner == chosen) | (owner == (partner + parts // 2) % parts)
    return jnp.where(strong, factor * array, array)


def block_scale(stream_key, extent, pieces, least, high):
    def one(dim, blocks):
        draws = jax.random.uniform(jax.random.fold_in(jax.random.fold_in(stream_key, 6), dim), (blocks,), jnp.float32, least / len(pieces), high / len(pieces))
        return jnp.repeat(jnp.exp(draws), extent[dim] // blocks).reshape((-1,) + (1,) * (len(extent) - dim - 1))

    factor_of = one(*pieces[0])
    for cut in pieces[1:]:
        factor_of = factor_of * one(*cut)
    return factor_of


def bell_draw(rng, dims, spread, most, pieces=(), kind=jnp.bfloat16):
    array = spread * jax.random.normal(rng, dims, jnp.float32)
    if pieces:
        array = array * block_scale(rng, dims, pieces, -0.22, 0.18)
    return jnp.clip(array, -most, most).astype(kind)


def noise_with(stream_key, extent, width, bound, cuts, heavy, kind=jnp.bfloat16):
    result = width * jax.random.normal(stream_key, extent, jnp.float32)
    if cuts:
        result = result * block_scale(stream_key, extent, cuts, -0.22, 0.18)
    return jnp.clip(strengthened(result, jax.random.fold_in(stream_key, 3), *heavy), -bound, bound).astype(kind)


def setup_inputs(seed: int = 0) -> dict:
    arg_keys = jax.random.split(jax.random.key(seed), 6)
    return {
        "inputs": bell_draw(arg_keys[0], (STREAMS, LENGTH, RESIDUAL_WIDTH), 1.0, 6.0, ((0, 8), (1, 32))),
        "offsets": draw_offsets(jax.random.fold_in(arg_keys[5], 71), 0),
        "conv_weight": bell_draw(arg_keys[2], (2, RESIDUAL_WIDTH, GATES), (2 * RESIDUAL_WIDTH) ** -0.5, 0.1875),
        "res_weight": bell_draw(arg_keys[3], (RESIDUAL_WIDTH, RESIDUAL_WIDTH), RESIDUAL_WIDTH ** -0.5, 0.25),
        "cotangent": noise_with(arg_keys[4], (STREAMS, LENGTH, RESIDUAL_WIDTH), 1.0, 6.0, ((0, 8), (1, 32)), (1, 2, 32, 2.75)),
    }


def one_group(inputs, offsets, cotangent, conv_weight, res_weight):
    retain_mask = (offsets >= DILATION_GAP)[:, None]
    delayed_input = jnp.concatenate([jnp.zeros((DILATION_GAP, RESIDUAL_WIDTH), jnp.bfloat16), inputs[:-DILATION_GAP]], 0)
    past_rows = jnp.where(retain_mask, delayed_input, jnp.zeros_like(delayed_input))
    pre_gate = jnp.dot(inputs, conv_weight[0], preferred_element_type=jnp.float32)
    pre_gate = pre_gate + jnp.dot(past_rows, conv_weight[1], preferred_element_type=jnp.float32)
    filt_act = jnp.tanh(pre_gate[:, :RESIDUAL_WIDTH])
    gate_act = jax.nn.sigmoid(pre_gate[:, RESIDUAL_WIDTH:])
    hidden = (filt_act * gate_act).astype(jnp.bfloat16)
    output = (inputs.astype(jnp.float32) + jnp.dot(hidden, res_weight, preferred_element_type=jnp.float32)).astype(jnp.bfloat16)
    d_hidden = jnp.dot(cotangent, res_weight.T, preferred_element_type=jnp.float32)
    d_filter = d_hidden * gate_act * (1.0 - filt_act * filt_act)
    d_gate = d_hidden * filt_act * gate_act * (1.0 - gate_act)
    d_pregate = jnp.concatenate([d_filter, d_gate], 1).astype(jnp.bfloat16)
    masked = jnp.where(retain_mask, d_pregate, jnp.zeros_like(d_pregate))
    prior_gradient = jnp.dot(masked, conv_weight[1].T, preferred_element_type=jnp.float32).astype(jnp.bfloat16)
    following_rows = jnp.concatenate([prior_gradient[DILATION_GAP:], jnp.zeros((DILATION_GAP, RESIDUAL_WIDTH), jnp.bfloat16)], 0)
    d_inputs = cotangent.astype(jnp.float32) + jnp.dot(d_pregate, conv_weight[0].T, preferred_element_type=jnp.float32)
    d_inputs = (d_inputs + following_rows.astype(jnp.float32)).astype(jnp.bfloat16)
    grad_now = jnp.dot(inputs.T, d_pregate, preferred_element_type=jnp.float32)
    grad_past = jnp.dot(past_rows.T, d_pregate, preferred_element_type=jnp.float32)
    grad_res = jnp.dot(hidden.T, cotangent, preferred_element_type=jnp.float32)
    return (output, d_inputs, jnp.stack([grad_now, grad_past]), grad_res)

def reference(inputs, offsets, conv_weight, res_weight, cotangent):

    def step_fn(carry, items):
        output, d_inputs, grad_conv, grad_res = one_group(items[0], items[1], items[2], conv_weight, res_weight)
        return ((carry[0] + grad_conv, carry[1] + grad_res), (output, d_inputs))
    start = (jnp.zeros((2, RESIDUAL_WIDTH, 2 * RESIDUAL_WIDTH), jnp.float32), jnp.zeros((RESIDUAL_WIDTH, RESIDUAL_WIDTH), jnp.float32))
    totals, streams = lax.scan(step_fn, start, (inputs, offsets, cotangent))
    grad_scale = 1.0 / math.sqrt(N_GRP * DEVICE_SAMPLES * N_SEQ)
    return (streams[0], streams[1], totals[0] * grad_scale, totals[1] * grad_scale)
```

```python
import math

import jax
import jax.numpy as jnp
from jax import lax
from jax.sharding import PartitionSpec as P

DILATION_GAP = 4096
F32 = jnp.float32
BF16 = jnp.bfloat16
NX, NY, NZ, NC = 4, 4, 8, 2


def shifted(value, axis, by):
    length = lax.axis_size(axis)
    pairs = [(i, i + by) for i in range(length) if 0 <= i + by < length]
    return lax.ppermute(value, axis, pairs)


def core_swap(value):
    return lax.ppermute(value, "grp", [(i, i ^ 1) for i in range(NY * NC)])


def y_turn(value, k):
    return lax.ppermute(
        value,
        "grp",
        [(y * NC + c, (y + k) % NY * NC + c) for y in range(NY) for c in range(NC)],
    )


def x_turn(value, k):
    return lax.ppermute(
        value,
        "seq",
        [(z * NX + x, z * NX + (x + k) % NX) for z in range(NZ) for x in range(NX)],
    )


def z_swap(value):
    return lax.ppermute(
        value, "seq", [(z * NX + x, (z ^ 1) * NX + x) for z in range(NZ) for x in range(NX)]
    )


def z_turn(value, k):
    return lax.ppermute(
        value,
        "seq",
        [(z * NX + x, (z + 2 * k) % NZ * NX + x) for z in range(NZ) for x in range(NX)],
    )


def pick(value, at):
    return lax.dynamic_index_in_dim(value, at, 0, keepdims=False)


def spread(value, at, turn, dtype):
    parts = [turn(pick(value, (at + k) % 4).astype(dtype), k) for k in (2, 1, 3)]
    total = pick(value, at)
    for part in parts:
        total = total + part.astype(F32)
    return total


def reduce_terms(now_t, past_t, res_t):
    grp, seq = lax.axis_index("grp"), lax.axis_index("seq")
    y, c = grp // NC, grp % NC
    z, x = seq // NX, seq % NX

    def blocks(value):
        rows = value.shape[0] // (NZ * NX * NC)
        cut = value.reshape(2, 4, NX, NC, rows, NY, 128).transpose(3, 0, 5, 2, 1, 4, 6)
        return cut.reshape(NC, 2, NY, NX, 4 * rows, 128)

    table = jnp.concatenate([blocks(now_t), blocks(past_t), blocks(res_t)], 4)
    got = core_swap(pick(table, 1 - c).astype(BF16))
    table = pick(table, c) + got.astype(F32)
    first = spread(table[0], y, y_turn, BF16)
    second = spread(table[1].swapaxes(0, 1), x, x_turn, BF16)
    first = spread(first, x, x_turn, F32)
    second = spread(second, y, y_turn, F32)

    def by_z(value):
        return jnp.concatenate(
            [value[:64].reshape(4, 16, 128), value[64:128].reshape(4, 16, 128), value[128:].reshape(4, 8, 128)], 1
        )

    pieces = jnp.concatenate([by_z(first), by_z(second)], 0).reshape(4, 2, 40, 128)
    pieces = pieces.swapaxes(0, 1)
    got = z_swap(pick(pieces, 1 - z % 2))
    pieces = pick(pieces, z % 2) + got
    piece = spread(pieces, z // 2, z_turn, F32)
    both = jnp.stack([piece, core_swap(piece)])
    both = jnp.where(c == 0, both, both[::-1])
    full = jnp.zeros((NY, NC, 40, 128), F32)
    full = lax.dynamic_update_index_in_dim(full, both, y, 0)
    for k in (2, 1, 3):
        full = lax.dynamic_update_index_in_dim(full, y_turn(both, k), (y - k) % NY, 0)
    full = full.transpose(1, 2, 0, 3).reshape(NC, 40, 512)
    now_rows = full[:, :16].reshape(32, 512)
    past_rows = full[:, 16:32].reshape(32, 512)
    res_rows = full[:, 32:].reshape(16, 512)
    return now_rows, past_rows, res_rows


def local(inputs, offsets, conv_weight, res_weight, cotangent):
    inputs_now = inputs[0]
    cot_rows = cotangent[0]
    count_of_rows = inputs_now.shape[0]
    chan_width = inputs_now.shape[1]
    jump_count = DILATION_GAP // count_of_rows
    retain_mask = (offsets[0] >= DILATION_GAP)[:, None]
    delayed_input = shifted(inputs_now, "seq", jump_count)
    past_rows = jnp.where(retain_mask, delayed_input, jnp.zeros_like(delayed_input))
    pre_gate = jnp.dot(inputs_now, conv_weight[0], preferred_element_type=F32)
    pre_gate = pre_gate + jnp.dot(past_rows, conv_weight[1], preferred_element_type=F32)
    filt_act = jnp.tanh(pre_gate[:, :chan_width])
    gate_act = jax.nn.sigmoid(pre_gate[:, chan_width:])
    hidden = (filt_act * gate_act).astype(BF16)
    output = (
        inputs_now.astype(F32) + jnp.dot(hidden, res_weight, preferred_element_type=F32)
    ).astype(BF16)
    d_hidden = jnp.dot(cot_rows, res_weight.T, preferred_element_type=F32)
    d_filter = d_hidden * gate_act * (1.0 - filt_act * filt_act)
    d_gate = d_hidden * filt_act * gate_act * (1.0 - gate_act)
    d_pregate = jnp.concatenate([d_filter, d_gate], 1).astype(BF16)
    masked = jnp.where(retain_mask, d_pregate, jnp.zeros_like(d_pregate))
    prior_gradient = jnp.dot(masked, conv_weight[1].T, preferred_element_type=F32).astype(BF16)
    following_rows = shifted(prior_gradient, "seq", -jump_count)
    current_grad = jnp.dot(d_pregate, conv_weight[0].T, preferred_element_type=F32)
    d_inputs = (cot_rows.astype(F32) + current_grad + following_rows.astype(F32)).astype(BF16)
    grad_scale = 1.0 / math.sqrt(lax.axis_size("grp") * lax.axis_size("seq") * count_of_rows)
    now_t = jnp.dot(d_pregate.T, inputs_now, preferred_element_type=F32) * grad_scale
    past_t = jnp.dot(d_pregate.T, past_rows, preferred_element_type=F32) * grad_scale
    res_t = jnp.dot(cot_rows.T, hidden, preferred_element_type=F32) * grad_scale
    now_sum, past_sum, res_sum = reduce_terms(now_t, past_t, res_t)
    d_conv = jnp.stack([now_sum.T, past_sum.T])
    return (output[None], d_inputs[None], d_conv, res_sum.T)


def solution(mesh):
    placed = (P("grp", "seq", None), P("grp", "seq"), P(), P(), P("grp", "seq", None))
    return jax.shard_map(
        local,
        mesh=mesh,
        in_specs=placed,
        out_specs=(
            P("grp", "seq", None),
            P("grp", "seq", None),
            P(None, None, "seq"),
            P(None, "seq"),
        ),
        check_vma=False,
    )
```

```python
import functools

import jax
import jax.numpy as jnp
from jax import lax
from jax.experimental import pallas as pl
from jax.experimental.pallas import tpu as pltpu
from jax.sharding import PartitionSpec as P

DILATION_GAP = 4096
F32 = jnp.float32
BF16 = jnp.bfloat16
NX, NY, NZ, NC = 4, 4, 8, 2
WIDTH = 512
ROWS = 1024
BLOCK = 256
EARLY = 768
VMEM_LIMIT = 56 * 1024 * 1024


def shape(dims, dtype):
    return jax.ShapeDtypeStruct(dims, dtype)


def whole(dims):
    return pl.BlockSpec(dims, lambda *_: (0,) * len(dims))


def params():
    return pltpu.CompilerParams(vmem_limit_bytes=VMEM_LIMIT)


def shifted(value, axis, by):
    length = lax.axis_size(axis)
    pairs = [(i, i + by) for i in range(length) if 0 <= i + by < length]
    return lax.ppermute(value, axis, pairs)


def grp_swap(value, j):
    return lax.ppermute(value, "grp", [(i, i ^ j) for i in range(NY * NC)])


def y_swap(value, j):
    return grp_swap(value, j * NC)


def seq_swap(value, j):
    return lax.ppermute(value, "seq", [(i, i ^ j) for i in range(NX * NZ)])


def x_swap(value, j):
    return seq_swap(value, j)


def z_swap(value, j):
    return seq_swap(value, j * NX)


def dot(a, b, contract):
    return lax.dot_general(a, b, (contract, ((), ())), preferred_element_type=F32)


NN = ((1,), (0,))
NT = ((1,), (1,))
TN = ((0,), (0,))


def layer_block(x_ref, past_ref, keep_ref, cot_ref, conv_ref, res_ref, out_ref, cur_ref, prior_ref):
    x, cot = x_ref[...], cot_ref[...]
    keep = jnp.concatenate([keep_ref[...]] * (WIDTH // 128), 1)
    past = past_ref[...] * keep
    w0, w1, wr = conv_ref[0], conv_ref[1], res_ref[...]
    pre = dot(x, w0, NN) + dot(past, w1, NN)
    filt = jnp.tanh(pre[:, :WIDTH])
    gate = jax.nn.sigmoid(pre[:, WIDTH:])
    hidden = (filt * gate).astype(BF16)
    d_hidden = dot(cot, wr, NT)
    d_filter = d_hidden * gate * (1.0 - filt * filt)
    d_gate = d_hidden * filt * gate * (1.0 - gate)
    d_pre = jnp.concatenate([d_filter.astype(BF16), d_gate.astype(BF16)], 1)
    out_ref[...] = (x.astype(F32) + dot(hidden, wr, NN)).astype(BF16)
    cur_ref[...] = cot.astype(F32) + dot(d_pre, w0, NT)
    prior_ref[...] = (dot(d_pre, w1, NT) * keep.astype(F32)).astype(BF16)
    return dot(d_pre, x, TN), dot(d_pre, past, TN), dot(cot, hidden, TN)


def early_kernel(x, past, keep, cot, conv, res, out, cur, prior, acc0, acc1, accr):
    terms = layer_block(x, past, keep, cot, conv, res, out, cur, prior)

    @pl.when(pl.program_id(0) == 0)
    def _():
        for acc, term in zip((acc0, acc1, accr), terms):
            acc[...] = term

    @pl.when(pl.program_id(0) > 0)
    def _():
        for acc, term in zip((acc0, acc1, accr), terms):
            acc[...] += term


def late_kernel(where, x, past, keep, cot, conv, res, sum0, sum1, sumr, _out, _cur, out, cur, prior, own, send, acc0, acc1, accr):
    terms = layer_block(x, past, keep, cot, conv, res, out, cur, prior)
    for acc, before, term in zip((acc0, acc1, accr), (sum0, sum1, sumr), terms):
        acc[...] = before[...] + term
    core = where[0]
    for side, table, dtype in ((core, own, F32), (1 - core, send, BF16)):
        for p in range(2):
            for s in range(4 * NX):
                z, x_at = s // NX, s % NX
                row = (p * 4 + z) * NX + x_at
                at = pl.ds(pl.multiple_of(row * 32 + side * 16, 16), 16)
                now, past_term = acc0[at, :], acc1[at, :]
                for y in range(NY):
                    lanes = slice(y * 128, y * 128 + 128)
                    slot = (p, y, x_at) if p == 0 else (p, x_at, y)
                    table[slot + (slice(z * 16, z * 16 + 16),)] = now[:, lanes].astype(dtype)
                    table[slot + (slice(64 + z * 16, 80 + z * 16),)] = past_term[:, lanes].astype(dtype)
            for pair in range(2 * NX):
                z, x_at = pair // NX * 2, pair % NX
                halves = []
                for i in range(2):
                    row = (p * 4 + z + i) * NX + x_at
                    halves.append(accr[pl.ds(pl.multiple_of(row * 16 + side * 8, 8), 8), :])
                both = jnp.concatenate(halves, 0)
                for y in range(NY):
                    slot = (p, y, x_at) if p == 0 else (p, x_at, y)
                    table[slot + (slice(128 + z * 8, 144 + z * 8),)] = both[:, y * 128 : y * 128 + 128].astype(dtype)


def rows_spec(first, width):
    return pl.BlockSpec((BLOCK, width), lambda i, *_: (first // BLOCK + i, 0))


def early_part(x, past, keep, cot, conv, res):
    at, here = functools.partial(rows_spec, 0), functools.partial(rows_spec, 0)
    big, small = (2 * WIDTH, WIDTH), (WIDTH, WIDTH)
    return pl.pallas_call(
        early_kernel,
        grid=(EARLY // BLOCK,),
        in_specs=[at(WIDTH), here(WIDTH), at(128), at(WIDTH), whole(conv.shape), whole(res.shape)],
        out_specs=[at(WIDTH), at(WIDTH), here(WIDTH), whole(big), whole(big), whole(small)],
        out_shape=[
            shape((ROWS, WIDTH), BF16),
            shape((ROWS, WIDTH), F32),
            shape((EARLY, WIDTH), BF16),
            shape(big, F32),
            shape(big, F32),
            shape(small, F32),
        ],
        compiler_params=params(),
        name="early_rows",
    )(x, past, keep, cot, conv, res)


def late_part(where, x, past, keep, cot, conv, res, sums, out, cur):
    at, here = functools.partial(rows_spec, EARLY), functools.partial(rows_spec, 0)
    big, small = (2 * WIDTH, WIDTH), (WIDTH, WIDTH)
    table = (2, 4, 4, 160, 128)
    anywhere = pl.BlockSpec(memory_space=pl.ANY)
    return pl.pallas_call(
        late_kernel,
        grid_spec=pltpu.PrefetchScalarGridSpec(
            num_scalar_prefetch=1,
            grid=((ROWS - EARLY) // BLOCK,),
            in_specs=[at(WIDTH), here(WIDTH), at(128), at(WIDTH), whole(conv.shape), whole(res.shape)]
            + [whole(big), whole(big), whole(small), anywhere, anywhere],
            out_specs=[at(WIDTH), at(WIDTH), here(WIDTH), whole(table), whole(table)],
            scratch_shapes=[pltpu.VMEM(big, F32), pltpu.VMEM(big, F32), pltpu.VMEM(small, F32)],
        ),
        out_shape=[
            shape((ROWS, WIDTH), BF16),
            shape((ROWS, WIDTH), F32),
            shape((ROWS - EARLY, WIDTH), BF16),
            shape(table, F32),
            shape(table, BF16),
        ],
        input_output_aliases={10: 0, 11: 1},
        compiler_params=params(),
        name="late_rows",
    )(where, x, past, keep, cot, conv, res, *sums, out, cur)


def call(kernel, where, args, outs, scratch=(), name=None):
    return pl.pallas_call(
        kernel,
        grid_spec=pltpu.PrefetchScalarGridSpec(
            num_scalar_prefetch=1,
            grid=(1,),
            in_specs=[whole(a.shape) for a in args],
            out_specs=[whole(o.shape) for o in outs],
            scratch_shapes=list(scratch),
        ),
        out_shape=list(outs),
        compiler_params=params(),
        name=name,
    )(where, *args)


def after_core(where, own, got, *outs):
    for p, me in ((0, where[1]), (1, where[2])):
        for j in range(4):
            at = me ^ j
            total = own[p, at] + got[p, at].astype(F32)
            outs[p * 4 + j][...] = total.astype(outs[p * 4 + j].dtype)


def after_first(side, where, own, one, two, three, *outs):
    me = where[side]
    for j in range(4):
        at = me ^ j
        outs[j][...] = own[at] + one[at].astype(F32) + two[at].astype(F32) + three[at].astype(F32)


def after_second(where, own_a, a1, a2, a3, own_b, b1, b2, b3, *rest):
    outs, pieces = rest[:8], rest[8]
    for p, refs in enumerate(((own_a, a1, a2, a3), (own_b, b1, b2, b3))):
        total = refs[0][...] + refs[1][...] + refs[2][...] + refs[3][...]
        for z in range(4):
            pieces[p * 4 + z, :16] = total[z * 16 : z * 16 + 16]
            pieces[p * 4 + z, 16:32] = total[64 + z * 16 : 80 + z * 16]
            pieces[p * 4 + z, 32:] = total[128 + z * 8 : 136 + z * 8]
    for j in range(8):
        outs[j][...] = pieces[where[3] ^ j]


def after_z(where, *refs):
    total = refs[0][...]
    for ref in refs[1:8]:
        total = total + ref[...]
    refs[8][...] = total * (1.0 / 512.0)


def assemble(where, *refs):
    conv, res, pieces = refs[8:]
    for j in range(8):
        pieces[j] = refs[j][...]
    for g in range(8):
        y, c = g // NC, g % NC
        piece = pieces[where[4] ^ g]
        lanes = slice(y * 128, y * 128 + 128)
        conv[0, c * 16 : c * 16 + 16, lanes] = piece[:16]
        conv[1, c * 16 : c * 16 + 16, lanes] = piece[16:32]
        res[c * 8 : c * 8 + 8, lanes] = piece[32:]


def reduce_terms(where, own, send):
    got = grp_swap(send, 1)
    half, quarter, piece = (4, 160, 128), (160, 128), (40, 128)
    outs = [shape(half, F32 if j == 0 else BF16) for _ in range(2) for j in range(4)]
    *a, b0, b1, b2, b3 = call(after_core, where, [own, got], outs, name="after_core")
    got_a = [y_swap(a[j], j) for j in (2, 1, 3)]
    got_b = [x_swap(b, j) for b, j in ((b2, 2), (b1, 1), (b3, 3))]
    outs = [shape(quarter, F32)] * 4
    a = call(functools.partial(after_first, 2), where, [a[0], *got_a], outs, name="after_first_a")
    b = call(functools.partial(after_first, 1), where, [b0, *got_b], outs, name="after_first_b")
    got_a = [x_swap(a[j], j) for j in (2, 1, 3)]
    got_b = [y_swap(b[j], j) for j in (2, 1, 3)]
    parts = call(
        after_second,
        where,
        [a[0], *got_a, b[0], *got_b],
        [shape(piece, F32)] * 8,
        [pltpu.VMEM((8,) + piece, F32)],
        name="after_second",
    )
    parts = [parts[0]] + [z_swap(parts[j], j) for j in (4, 3, 5, 2, 6, 1, 7)]
    (mine,) = call(after_z, where, parts, [shape(piece, F32)], name="after_z")
    parts = [mine] + [grp_swap(mine, j) for j in range(1, 8)]
    conv, res = call(
        assemble,
        where,
        parts,
        [shape((2, 32, WIDTH), F32), shape((16, WIDTH), F32)],
        [pltpu.VMEM((8,) + piece, F32)],
        name="assemble",
    )
    return conv.swapaxes(1, 2), res.T


def local(inputs, offsets, conv_weight, res_weight, cotangent):
    x, cot = inputs[0], cotangent[0]
    jump = DILATION_GAP // ROWS
    grp, seq = lax.axis_index("grp"), lax.axis_index("seq")
    where = jnp.stack([grp % NC, grp // NC, seq % NX, seq // NX, grp]).astype(jnp.int32)
    past_early = shifted(x[:EARLY], "seq", jump)
    past_late = shifted(x[EARLY:], "seq", jump)
    keep = jnp.broadcast_to((offsets[0] >= DILATION_GAP).astype(BF16)[:, None], (ROWS, 128))
    out, cur, prior_early, *sums = early_part(x, past_early, keep, cot, conv_weight, res_weight)
    next_early = shifted(prior_early, "seq", -jump)
    out, cur, prior_late, own, send = late_part(
        where, x, past_late, keep, cot, conv_weight, res_weight, sums, out, cur
    )
    next_late = shifted(prior_late, "seq", -jump)
    d_conv, d_res = reduce_terms(where, own, send)
    following = jnp.concatenate([next_early, next_late], 0)
    d_inputs = (cur + following.astype(F32)).astype(BF16)
    return (out[None], d_inputs[None], d_conv, d_res)


def solution(mesh):
    placed = (P("grp", "seq", None), P("grp", "seq"), P(), P(), P("grp", "seq", None))
    return jax.shard_map(
        local,
        mesh=mesh,
        in_specs=placed,
        out_specs=(
            P("grp", "seq", None),
            P("grp", "seq", None),
            P(None, None, "seq"),
            P(None, "seq"),
        ),
        check_vma=False,
    )
```

```python
import functools

import jax
import jax.numpy as jnp
from jax import lax
from jax.experimental import pallas as pl
from jax.experimental.pallas import tpu as pltpu
from jax.sharding import PartitionSpec as P

DILATION_GAP = 4096
F32 = jnp.float32
BF16 = jnp.bfloat16
NX, NY, NZ, NC = 4, 4, 8, 2
WIDTH = 512
ROWS = 1024
BLOCK = 256
PARTS = ((0, 256), (256, 256), (512, 256), (768, 256))
EARLY = PARTS[-1][0]
TABLE = (2, 4, 4, 160, 128)
BIG, SMALL = (2 * WIDTH, WIDTH), (WIDTH, WIDTH)
HALF, QUARTER, PIECE = (4, 160, 128), (160, 128), (40, 128)
VMEM_LIMIT = 24 * 1024 * 1024

NN = ((1,), (0,))
NT = ((1,), (1,))
TN = ((0,), (0,))


def shifted(value, axis, by):
    length = lax.axis_size(axis)
    pairs = [(i, i + by) for i in range(length) if 0 <= i + by < length]
    return lax.ppermute(value, axis, pairs)


def grp_swap(value, j):
    return lax.ppermute(value, "grp", [(i, i ^ j) for i in range(NY * NC)])


def y_swap(value, j):
    return grp_swap(value, j * NC)


def x_swap(value, j):
    return lax.ppermute(value, "seq", [(i, i ^ j) for i in range(NX * NZ)])


def z_swap(value, j):
    return x_swap(value, j * NX)


def call(kernel, name, args, outs, where=None, scratch=(), aliases=None):
    here = pl.BlockSpec(memory_space=pltpu.VMEM)
    lead = [] if where is None else [where]
    return pl.pallas_call(
        kernel,
        in_specs=[pl.BlockSpec(memory_space=pltpu.SMEM)] * len(lead) + [here] * len(args),
        out_specs=[here] * len(outs),
        out_shape=[pltpu.VMEM(dims, dtype) for dims, dtype in outs],
        scratch_shapes=[pltpu.VMEM(dims, dtype) for dims, dtype in scratch],
        input_output_aliases={len(lead) + i: o for i, o in (aliases or {}).items()},
        compiler_params=pltpu.CompilerParams(vmem_limit_bytes=VMEM_LIMIT),
        name=name,
    )(*lead, *[pltpu.with_memory_space_constraint(a, pltpu.VMEM) for a in args])


def dot(a, b, contract):
    return lax.dot_general(a, b, (contract, ((), ())), preferred_element_type=F32)


def layer_block(rows, at, back, x_ref, past_ref, keep_ref, cot_ref, conv_ref, res_ref, out_ref, cur_ref, prior_ref):
    x, cot = x_ref[rows, :], cot_ref[rows, :]
    keep = jnp.concatenate([keep_ref[rows, :]] * (WIDTH // 128), 1)
    past = past_ref[at, :] * keep
    w0, w1, wr = conv_ref[0], conv_ref[1], res_ref[...]
    pre = dot(x, w0, NN) + dot(past, w1, NN)
    filt = jnp.tanh(pre[:, :WIDTH])
    gate = jax.nn.sigmoid(pre[:, WIDTH:])
    hidden = (filt * gate).astype(BF16)
    d_hidden = dot(cot, wr, NT)
    d_filter = d_hidden * gate * (1.0 - filt * filt)
    d_gate = d_hidden * filt * gate * (1.0 - gate)
    d_pre = jnp.concatenate([d_filter.astype(BF16), d_gate.astype(BF16)], 1)
    out_ref[rows, :] = (x.astype(F32) + dot(hidden, wr, NN)).astype(BF16)
    cur_ref[rows, :] = cot.astype(F32) + dot(d_pre, w0, NT)
    prior_ref[back, :] = (dot(d_pre, w1, NT) * keep.astype(F32)).astype(BF16)
    return dot(d_pre, x, TN), dot(d_pre, past, TN), dot(cot, hidden, TN)


def layer_rows(part, ins, outs, sums, fresh):
    lo, count = part
    base = EARLY if lo == EARLY else 0
    for i in range(0, count, BLOCK):
        rows, at = pl.ds(lo + i, BLOCK), pl.ds(i, BLOCK)
        terms = layer_block(rows, at, pl.ds(lo + i - base, BLOCK), *ins, *outs)
        for total, term in zip(sums, terms):
            if fresh and i == 0:
                total[...] = term
            else:
                total[...] += term


def first_kernel(part, *refs):
    layer_rows(part, refs[:6], refs[6:9], refs[9:], True)


def next_kernel(part, *refs):
    layer_rows(part, refs[:6], refs[12:15], refs[15:], False)


def last_kernel(part, where, *refs):
    ins, (out, cur, *sums, prior, own, send) = refs[:6], refs[11:]
    layer_rows(part, ins, (out, cur, prior), sums, False)
    acc0, acc1, accr = sums
    core = where[0]
    for side, table, dtype in ((1 - core, send, BF16), (core, own, F32)):
        for p in range(2):
            for s in range(4 * NX):
                z, x_at = s // NX, s % NX
                row = (p * 4 + z) * NX + x_at
                at = pl.ds(pl.multiple_of(row * 32 + side * 16, 16), 16)
                now, past = acc0[at, :], acc1[at, :]
                for y in range(NY):
                    lanes = slice(y * 128, y * 128 + 128)
                    slot = (p, y, x_at) if p == 0 else (p, x_at, y)
                    table[slot + (slice(z * 16, z * 16 + 16),)] = now[:, lanes].astype(dtype)
                    table[slot + (slice(64 + z * 16, 80 + z * 16),)] = past[:, lanes].astype(dtype)
            for pair in range(2 * NX):
                z, x_at = pair // NX * 2, pair % NX
                halves = []
                for i in range(2):
                    row = (p * 4 + z + i) * NX + x_at
                    halves.append(accr[pl.ds(pl.multiple_of(row * 16 + side * 8, 8), 8), :])
                both = jnp.concatenate(halves, 0)
                for y in range(NY):
                    slot = (p, y, x_at) if p == 0 else (p, x_at, y)
                    table[slot + (slice(128 + z * 8, 144 + z * 8),)] = both[:, y * 128 : y * 128 + 128].astype(dtype)


def layer(where, x, pasts, keep, cot, conv, res):
    full = ((ROWS, WIDTH), BF16), ((ROWS, WIDTH), F32)
    totals = (BIG, F32), (BIG, F32), (SMALL, F32)
    early = ((EARLY, WIDTH), BF16)
    state = call(
        functools.partial(first_kernel, PARTS[0]), "layer_first", [x, pasts[0], keep, cot, conv, res], [*full, early, *totals]
    )
    for i in range(1, len(PARTS) - 1):
        state = call(
            functools.partial(next_kernel, PARTS[i]),
            "layer_next",
            [x, pasts[i], keep, cot, conv, res, *state],
            [*full, early, *totals],
            aliases={6 + j: j for j in range(6)},
        )
    out, cur, prior_early, *sums = state
    out, cur, _, _, _, prior_late, own, send = call(
        functools.partial(last_kernel, PARTS[-1]),
        "layer_last",
        [x, pasts[-1], keep, cot, conv, res, out, cur, *sums],
        [*full, *totals, ((ROWS - EARLY, WIDTH), BF16), (TABLE, F32), (TABLE, BF16)],
        where,
        aliases={6 + j: j for j in range(5)},
    )
    return out, cur, prior_early, prior_late, own, send


def after_core(where, own, got, *outs):
    for p, me in ((0, where[1]), (1, where[2])):
        for j in (2, 1, 3, 0):
            at = me ^ j
            total = own[p, at] + got[p, at].astype(F32)
            outs[p * 4 + j][...] = total.astype(outs[p * 4 + j].dtype)


def after_first(side, where, own, one, two, three, *outs):
    me = where[side]
    for j in range(4):
        at = me ^ j
        outs[j][...] = own[at] + one[at].astype(F32) + two[at].astype(F32) + three[at].astype(F32)


def after_second(where, *refs):
    keep, send, pieces = refs[8:]
    for p in range(2):
        a, b, c, d = refs[p * 4 : p * 4 + 4]
        total = a[...] + b[...] + c[...] + d[...]
        for z in range(4):
            pieces[p * 4 + z, :16] = total[z * 16 : z * 16 + 16]
            pieces[p * 4 + z, 16:32] = total[64 + z * 16 : 80 + z * 16]
            pieces[p * 4 + z, 32:] = total[128 + z * 8 : 136 + z * 8]
    odd = where[3] & 1
    for i in range(4):
        keep[i] = pieces[2 * i + odd]
        send[i] = pieces[2 * i + 1 - odd]


def after_z_pair(where, keep, got, *outs):
    me = where[3] >> 1
    for j in range(4):
        outs[j][...] = keep[me ^ j] + got[me ^ j]


def after_z(a, b, c, d, out):
    out[...] = (a[...] + b[...] + c[...] + d[...]) * (1.0 / 512.0)


def join(where, mine, got, both):
    both[where[0]] = mine[...]
    both[1 - where[0]] = got[...]


def assemble(where, *refs):
    conv, res, table = refs[4:]
    for j in range(4):
        table[j] = refs[j][...]
    for y in range(NY):
        pair = table[where[1] ^ y]
        lanes = slice(y * 128, y * 128 + 128)
        for c in range(NC):
            conv[0, c * 16 : c * 16 + 16, lanes] = pair[c, :16]
            conv[1, c * 16 : c * 16 + 16, lanes] = pair[c, 16:32]
            res[c * 8 : c * 8 + 8, lanes] = pair[c, 32:]


def reduce_terms(where, own, send):
    got = grp_swap(send, 1)
    outs = [(HALF, F32 if j == 0 else BF16) for _ in range(2) for j in range(4)]
    sides = call(after_core, "after_core", [own, got], outs, where)
    a, b = sides[:4], sides[4:]
    got_a, got_b = {}, {}
    for j in (2, 1, 3):
        got_a[j] = y_swap(a[j], j)
        got_b[j] = x_swap(b[j], j)
    outs = [(QUARTER, F32)] * 4
    a = call(functools.partial(after_first, 2), "after_first_a", [a[0], got_a[1], got_a[2], got_a[3]], outs, where)
    b = call(functools.partial(after_first, 1), "after_first_b", [b[0], got_b[1], got_b[2], got_b[3]], outs, where)
    for j in (2, 1, 3):
        got_a[j] = x_swap(a[j], j)
        got_b[j] = y_swap(b[j], j)
    eight = (8,) + PIECE
    four = (4,) + PIECE
    keep, send = call(
        after_second,
        "after_second",
        [a[0], got_a[1], got_a[2], got_a[3], b[0], got_b[1], got_b[2], got_b[3]],
        [(four, F32), (four, F32)],
        where,
        [(eight, F32)],
    )
    parts = call(after_z_pair, "after_z_pair", [keep, z_swap(send, 1)], [(PIECE, F32)] * 4, where)
    parts = [parts[0]] + [z_swap(parts[j], 2 * j) for j in (2, 1, 3)]
    (mine,) = call(after_z, "after_z", parts, [(PIECE, F32)])
    (both,) = call(join, "join", [mine, grp_swap(mine, 1)], [((2,) + PIECE, F32)], where)
    table = {0: both}
    for j in (2, 1, 3):
        table[j] = y_swap(both, j)
    conv, res = call(
        assemble,
        "assemble",
        [table[j] for j in range(4)],
        [((2, 32, WIDTH), F32), ((16, WIDTH), F32)],
        where,
        [((4, 2) + PIECE, F32)],
    )
    return conv.swapaxes(1, 2), res.T


def local(inputs, offsets, conv_weight, res_weight, cotangent):
    x, cot = inputs[0], cotangent[0]
    jump = DILATION_GAP // ROWS
    grp, seq = lax.axis_index("grp"), lax.axis_index("seq")
    where = jnp.stack([grp & 1, grp >> 1, seq & 3, seq >> 2]).astype(jnp.int32)
    pasts = [shifted(x[lo : lo + count], "seq", jump) for lo, count in PARTS]
    keep = jnp.broadcast_to((offsets[0] >= DILATION_GAP).astype(BF16)[:, None], (ROWS, 128))
    out, cur, prior_early, prior_late, own, send = layer(where, x, pasts, keep, cot, conv_weight, res_weight)
    next_early = shifted(prior_early, "seq", -jump)
    next_late = shifted(prior_late, "seq", -jump)
    d_conv, d_res = reduce_terms(where, own, send)
    following = jnp.concatenate([next_early, next_late], 0)
    d_inputs = (cur + following.astype(F32)).astype(BF16)
    return (out[None], d_inputs[None], d_conv, d_res)


def solution(mesh):
    placed = (P("grp", "seq", None), P("grp", "seq"), P(), P(), P("grp", "seq", None))
    return jax.shard_map(
        local,
        mesh=mesh,
        in_specs=placed,
        out_specs=(
            P("grp", "seq", None),
            P("grp", "seq", None),
            P(None, None, "seq"),
            P(None, "seq"),
        ),
        check_vma=False,
    )
```

```python
import functools

import jax
import jax.numpy as jnp
from jax import lax
from jax.experimental import pallas as pl
from jax.experimental.pallas import tpu as pltpu
from jax.sharding import PartitionSpec as P

DILATION_GAP = 4096
F32 = jnp.float32
BF16 = jnp.bfloat16
NX, NY, NZ, NC = 4, 4, 8, 2
WIDTH = 512
ROWS = 1024
BLOCK = 256
PARTS = ((0, 256), (256, 256), (512, 256), (768, 256))
AHEAD = 2
EARLY = PARTS[-1][0]
TABLE = (2, 4, 4, 160, 128)
BIG, SMALL = (2 * WIDTH, WIDTH), (WIDTH, WIDTH)
HALF, PIECE = (4, 160, 128), (40, 128)
MIB = 1024 * 1024

NN = ((1,), (0,))
NT = ((1,), (1,))
TN = ((0,), (0,))


def shifted(value, by):
    return lax.ppermute(value, "seq", [(i, (i + by) % (NX * NZ)) for i in range(NX * NZ)])


def grp_swap(value, j):
    return lax.ppermute(value, "grp", [(i, i ^ j) for i in range(NY * NC)])


def y_swap(value, j):
    return grp_swap(value, j * NC)


def call(kernel, name, args, outs, where=None, scratch=(), aliases=None, far=(), free_outs=False, far_outs=False, limit=4):
    here, there = pl.BlockSpec(memory_space=pltpu.VMEM), pl.BlockSpec(memory_space=pltpu.HBM)
    lead = [] if where is None else [where]
    return pl.pallas_call(
        kernel,
        in_specs=[pl.BlockSpec(memory_space=pltpu.SMEM)] * len(lead)
        + [there if i in far else here for i in range(len(args))],
        out_specs=[there if far_outs else here] * len(outs),
        out_shape=[(pltpu.HBM if far_outs else jax.ShapeDtypeStruct if free_outs else pltpu.VMEM)(*out) for out in outs],
        scratch_shapes=list(scratch),
        input_output_aliases={len(lead) + i: o for i, o in (aliases or {}).items()},
        compiler_params=pltpu.CompilerParams(vmem_limit_bytes=limit * MIB),
        name=name,
    )(*lead, *[pltpu.with_memory_space_constraint(a, pltpu.HBM if i in far else pltpu.VMEM) for i, a in enumerate(args)])


def dot(a, b, contract):
    return lax.dot_general(a, b, (contract, ((), ())), preferred_element_type=F32)


def stage(pairs, sems):
    copies = [pltpu.make_async_copy(src, dst, sems.at[i]) for i, (src, dst) in enumerate(pairs)]
    for copy in copies:
        copy.start()
    for copy in copies:
        copy.wait()


def flush(out, far, sems):
    stage([(out, far)], sems)


def stage_one(part, x, *rest):
    chunk, sems = rest[-2:]
    stage([(x.at[pl.ds(*part)], chunk)], sems)


def stage_rest(x, cot, conv, res, _first, x_out, cot_out, conv_out, res_out, *rest):
    chunks, sems = rest[:-1], rest[-1]
    pairs = [(x.at[pl.ds(lo, count)], chunk) for (lo, count), chunk in zip(PARTS[AHEAD:], chunks)]
    stage(pairs + [(x, x_out), (conv, conv_out), (cot, cot_out), (res, res_out)], sems)


def load(x, cot, conv, res):
    outs = [((count, WIDTH), BF16) for _, count in PARTS]
    ahead = []
    for part, out in zip(PARTS[:AHEAD], outs):
        kernel = functools.partial(stage_one, part)
        ahead += call(kernel, "stage_one", [x, *ahead], [out], far=(0,), scratch=[pltpu.SemaphoreType.DMA((1,))])
    outs = [(a.shape, BF16) for a in (x, cot, conv, res)] + outs[AHEAD:]
    x, cot, conv, res, *chunks = call(
        stage_rest,
        "stage_rest",
        [x, cot, conv, res, ahead[-1]],
        outs,
        far=(0, 1, 2, 3),
        scratch=[pltpu.SemaphoreType.DMA((len(outs),))],
    )
    return x, cot, conv, res, [*ahead, *chunks]


def layer_block(rows, at, back, x_ref, past_ref, keep_ref, cot_ref, conv_ref, res_ref, out_ref, cur_ref, prior_ref):
    x, cot = x_ref[rows, :], cot_ref[rows, :]
    keep = jnp.concatenate([keep_ref[rows, :]] * (WIDTH // 128), 1)
    past = past_ref[at, :] * keep
    w0, w1, wr = conv_ref[0], conv_ref[1], res_ref[...]
    pre = dot(x, w0, NN) + dot(past, w1, NN)
    filt = jnp.tanh(pre[:, :WIDTH])
    gate = jax.nn.sigmoid(pre[:, WIDTH:])
    hidden = (filt * gate).astype(BF16)
    d_hidden = dot(cot, wr, NT)
    d_filter = d_hidden * gate * (1.0 - filt * filt)
    d_gate = d_hidden * filt * gate * (1.0 - gate)
    d_pre = jnp.concatenate([d_filter.astype(BF16), d_gate.astype(BF16)], 1)
    out_ref[rows, :] = (x.astype(F32) + dot(hidden, wr, NN)).astype(BF16)
    cur_ref[rows, :] = cot.astype(F32) + dot(d_pre, w0, NT)
    prior_ref[back, :] = (dot(d_pre, w1, NT) * keep.astype(F32)).astype(BF16)
    return dot(d_pre, x, TN), dot(d_pre, past, TN), dot(cot, hidden, TN)


def layer_rows(part, ins, out, cur, prior, sums, fresh):
    lo, count = part
    base = EARLY if lo == EARLY else 0
    for i in range(0, count, BLOCK):
        size = min(BLOCK, count - i)
        terms = layer_block(pl.ds(lo + i, size), pl.ds(i, size), pl.ds(lo + i - base, size), *ins, out, cur, prior)
        for total, term in zip(sums, terms):
            if fresh and i == 0:
                total[...] = term
            else:
                total[...] += term


def first_kernel(part, *refs):
    ins, (out, cur, *sums, prior) = refs[:6], refs[6:]
    layer_rows(part, ins, out, cur, prior, sums, True)


def next_kernel(part, *refs):
    ins, (out, cur, *sums, prior) = refs[:6], refs[12:]
    layer_rows(part, ins, out, cur, prior, sums, False)


def last_kernel(part, where, *refs):
    ins, (out, cur, *sums, prior, own, send) = refs[:6], refs[11:]
    layer_rows(part, ins, out, cur, prior, sums, False)
    acc0, acc1, accr = sums
    core = where[0]
    for side, table in ((1 - core, send), (core, own)):
        for p in range(2):
            for s in range(4 * NX):
                z, x_at = s // NX, s % NX
                row = (p * 4 + z) * NX + x_at
                at = pl.ds(pl.multiple_of(row * 32 + side * 16, 16), 16)
                now, past = acc0[at, :], acc1[at, :]
                for y in range(NY):
                    lanes = slice(y * 128, y * 128 + 128)
                    slot = (p, y, x_at)
                    table[slot + (slice(z * 16, z * 16 + 16),)] = now[:, lanes]
                    table[slot + (slice(64 + z * 16, 80 + z * 16),)] = past[:, lanes]
            for pair in range(2 * NX):
                z, x_at = pair // NX * 2, pair % NX
                halves = []
                for i in range(2):
                    row = (p * 4 + z + i) * NX + x_at
                    halves.append(accr[pl.ds(pl.multiple_of(row * 16 + side * 8, 8), 8), :])
                both = jnp.concatenate(halves, 0)
                for y in range(NY):
                    slot = (p, y, x_at)
                    table[slot + (slice(128 + z * 8, 144 + z * 8),)] = both[:, y * 128 : y * 128 + 128]


def layer(where, x, pasts, keep, cot, conv, res):
    state = []
    for i, part in enumerate(PARTS):
        first, last = i == 0, i == len(PARTS) - 1
        outs = [((ROWS, WIDTH), BF16), ((ROWS, WIDTH), F32), (BIG, F32), (BIG, F32), (SMALL, F32)]
        if last:
            *state, early = state
            outs += [((ROWS - EARLY, WIDTH), BF16), (TABLE, F32), (TABLE, F32)]
        else:
            outs += [((EARLY, WIDTH), BF16)]
        kernel = first_kernel if first else last_kernel if last else next_kernel
        state = call(
            functools.partial(kernel, part),
            "layer_first" if first else "layer_last" if last else "layer_next",
            [x, pasts[i], keep, cot, conv, res, *state],
            outs,
            where if last else None,
            aliases={6 + j: j for j in range(len(state))},
            limit=24,
        )
    out, cur, _, _, _, late, own, send = state
    return out, cur, [early, late], own, send


def after_core(where, own, got, *outs):
    y = where[1]
    for p, (near, far) in enumerate(((1, 3), (3, 1))):
        keep, send = outs[2 * p], outs[2 * p + 1]
        for i, (stay, leave) in enumerate(((0, near), (far, 2))):
            keep[i] = own[p, y ^ stay] + got[p, y ^ stay]
            send[i] = (own[p, y ^ leave] + got[p, y ^ leave]).astype(BF16)


def after_y(keep0, got0, keep1, got1, _out, own0, send0, own1, send1):
    for keep, got, own, send in ((keep0, got0, own0, send0), (keep1, got1, own1, send1)):
        own[...] = keep[0] + got[0].astype(F32)
        send[...] = (keep[1] + got[1].astype(F32)).astype(BF16)


def before_seq(own0, got0, own1, got1, *rest):
    blocks = rest[-1]
    for p, (own, got) in enumerate(((own0, got0), (own1, got1))):
        for x in range(NX):
            total = own[x] + got[x].astype(F32)
            for z in range(4):
                rows = (total[z * 16 : z * 16 + 16], total[64 + z * 16 : 80 + z * 16], total[128 + z * 8 : 136 + z * 8])
                blocks[(p * 4 + z) * NX + x] = jnp.concatenate(rows, 0).astype(BF16)


def after_seq(pieces, _late, out):
    total = pieces[0].astype(F32)
    for i in range(1, NX * NZ):
        total = total + pieces[i].astype(F32)
    out[...] = total * (1.0 / 512.0)


def join(where, mine, got, both):
    both[where[0]] = mine[...]
    both[1 - where[0]] = got[...]


def assemble(where, *refs):
    conv, res, table = refs[4:]
    for j in range(4):
        table[j] = refs[j][...]
    for y in range(NY):
        pair = table[where[1] ^ y]
        lanes = slice(y * 128, y * 128 + 128)
        for c in range(NC):
            conv[0, c * 16 : c * 16 + 16, lanes] = pair[c, :16]
            conv[1, c * 16 : c * 16 + 16, lanes] = pair[c, 16:32]
            res[c * 8 : c * 8 + 8, lanes] = pair[c, 32:]


def reduce_terms(where, own, send, following, out):
    got = grp_swap(send, 1)
    pair, half = (2,) + HALF, HALF
    keep0, send0, keep1, send1 = call(after_core, "after_core", [own, got], [(pair, F32), (pair, BF16)] * 2, where, limit=8)
    got0, got1 = y_swap(send0, 1), y_swap(send1, 3)
    own0, send0, own1, send1 = call(after_y, "after_y", [keep0, got0, keep1, got1, out], [(half, F32), (half, BF16)] * 2, far=(4,))
    got0, got1 = y_swap(send0, 3), y_swap(send1, 1)
    (blocks,) = call(before_seq, "before_seq", [own0, got0, own1, got1, *following[:-1]], [((NX * NZ,) + PIECE, BF16)])
    pieces = lax.all_to_all(blocks, "seq", 0, 0)
    (mine,) = call(after_seq, "after_seq", [pieces, *following[-1:]], [(PIECE, F32)])
    (both,) = call(join, "join", [mine, grp_swap(mine, 1)], [((2,) + PIECE, F32)], where)
    table = {0: both}
    for j in (2, 1, 3):
        table[j] = y_swap(both, j)
    conv, res = call(
        assemble,
        "assemble",
        [table[j] for j in range(4)],
        [((2, 32, WIDTH), F32), ((16, WIDTH), F32)],
        where,
        [pltpu.VMEM((4, 2) + PIECE, F32)],
        free_outs=True,
    )
    return conv.swapaxes(1, 2), res.T


def local(inputs, offsets, conv_weight, res_weight, cotangent):
    x, cot = inputs[0], cotangent[0]
    jump = DILATION_GAP // ROWS
    grp, seq = lax.axis_index("grp"), lax.axis_index("seq")
    where = jnp.stack([grp & 1, grp >> 1, seq & 3, seq >> 2]).astype(jnp.int32)
    x, cot, conv_weight, res_weight, chunks = load(x, cot, conv_weight, res_weight)
    pasts = [shifted(chunk, jump) for chunk in chunks]
    keep = jnp.broadcast_to((offsets[0] >= DILATION_GAP).astype(BF16)[:, None], (ROWS, 128))
    out, cur, priors, own, send = layer(where, x, pasts, keep, cot, conv_weight, res_weight)
    following = [shifted(prior, -jump) for prior in priors]
    (out,) = call(flush, "flush", [out], [((ROWS, WIDTH), BF16)], scratch=[pltpu.SemaphoreType.DMA((1,))], far_outs=True)
    d_conv, d_res = reduce_terms(where, own, send, following, out)
    d_inputs = (cur + jnp.concatenate(following, 0).astype(F32)).astype(BF16)
    return (out[None], d_inputs[None], d_conv, d_res)


def solution(mesh):
    placed = (P("grp", "seq", None), P("grp", "seq"), P(), P(), P("grp", "seq", None))
    return jax.shard_map(
        local,
        mesh=mesh,
        in_specs=placed,
        out_specs=(
            P("grp", "seq", None),
            P("grp", "seq", None),
            P(None, None, "seq"),
            P(None, "seq"),
        ),
        check_vma=False,
    )
```

```python
import functools

import jax
import jax.numpy as jnp
from jax import lax
from jax.experimental import pallas as pl
from jax.experimental.pallas import tpu as pltpu
from jax.sharding import PartitionSpec as P

DILATION_GAP = 4096
F32 = jnp.float32
BF16 = jnp.bfloat16
NX, NY, NZ, NC = 4, 4, 8, 2
WIDTH = 512
ROWS = 1024
FIRST = 256
PARTS = ((256, 256), (512, 256), (768, 256))
TABLE = (2, 4, 4, 160, 128)
BIG, SMALL = (2 * WIDTH, WIDTH), (WIDTH, WIDTH)
HALF, PIECE = (4, 160, 128), (40, 128)
MIB = 1024 * 1024

NN = ((1,), (0,))
NT = ((1,), (1,))
TN = ((0,), (0,))


def shifted(value, by):
    return lax.ppermute(value, "seq", [(i, (i + by) % (NX * NZ)) for i in range(NX * NZ)])


def grp_swap(value, j):
    return lax.ppermute(value, "grp", [(i, i ^ j) for i in range(NY * NC)])


def y_swap(value, j):
    return grp_swap(value, j * NC)


def call(kernel, name, args, outs, where=None, scratch=(), aliases=None, far=(), free_outs=False, far_outs=False, limit=2):
    here, there = pl.BlockSpec(memory_space=pltpu.VMEM), pl.BlockSpec(memory_space=pltpu.HBM)
    lead = [] if where is None else [where]
    return pl.pallas_call(
        kernel,
        in_specs=[pl.BlockSpec(memory_space=pltpu.SMEM)] * len(lead)
        + [there if i in far else here for i in range(len(args))],
        out_specs=[there if far_outs else here] * len(outs),
        out_shape=[(pltpu.HBM if far_outs else jax.ShapeDtypeStruct if free_outs else pltpu.VMEM)(*out) for out in outs],
        scratch_shapes=list(scratch),
        input_output_aliases={len(lead) + i: o for i, o in (aliases or {}).items()},
        compiler_params=pltpu.CompilerParams(vmem_limit_bytes=limit * MIB),
        name=name,
    )(*lead, *[pltpu.with_memory_space_constraint(a, pltpu.HBM if i in far else pltpu.VMEM) for i, a in enumerate(args)])


def dot(a, b, contract):
    return lax.dot_general(a, b, (contract, ((), ())), preferred_element_type=F32)


def stage(pairs, sems):
    copies = [pltpu.make_async_copy(src, dst, sems.at[i]) for i, (src, dst) in enumerate(pairs)]
    for copy in copies:
        copy.start()
    for copy in copies:
        copy.wait()


def flush(out, far, sems):
    stage([(out, far)], sems)


def in_four(source, lo, count, result, at=0):
    step = count // 4
    return [(source.at[pl.ds(lo + i, step)], result.at[pl.ds(at + i, step)]) for i in range(0, count, step)]


def split_kernel(keep, x, cot, *refs):
    chunks, mine, sems = refs[:-2], refs[-2], refs[-1]
    pairs = []
    for part, chunk in zip(PARTS, chunks):
        pairs += in_four(x, *part, chunk)
    pairs += in_four(x, 0, FIRST, mine) + in_four(cot, 0, FIRST, mine, FIRST)
    stage(pairs + [(keep, mine.at[pl.ds(2 * FIRST, FIRST // 4)])], sems)


def split(keep, x, cot):
    outs = [((count, WIDTH), BF16) for _, count in PARTS] + [((2 * FIRST + FIRST // 4, WIDTH), BF16)]
    step = FIRST // 4
    wide = jnp.concatenate([keep[i : i + step] for i in range(0, FIRST, step)], 1)
    sems = [pltpu.SemaphoreType.DMA((4 * len(PARTS) + 9,))]
    return call(split_kernel, "split_rows", [wide, x, cot], outs, far=(1, 2), scratch=sems)


def gates(x, past, cot, conv_ref, res_ref):
    pre = dot(x, conv_ref[0], NN) + dot(past, conv_ref[1], NN)
    filt = jnp.tanh(pre[:, :WIDTH])
    gate = jax.nn.sigmoid(pre[:, WIDTH:])
    hidden = (filt * gate).astype(BF16)
    d_hidden = dot(cot, res_ref[...], NT)
    d_filter = d_hidden * gate * (1.0 - filt * filt)
    d_gate = d_hidden * filt * gate * (1.0 - gate)
    return hidden, jnp.concatenate([d_filter.astype(BF16), d_gate.astype(BF16)], 1)


def widened(keep):
    return jnp.concatenate([keep] * (WIDTH // 128), 1)


def results(rows, x, cot, hidden, d_pre, conv_ref, res_ref, out_ref, cur_ref):
    out_ref[rows, :] = (x.astype(F32) + dot(hidden, res_ref[...], NN)).astype(BF16)
    cur_ref[rows, :] = cot.astype(F32) + dot(d_pre, conv_ref[0], NT)


def past_grads(d_pre, keep, conv_ref):
    return (dot(d_pre, conv_ref[1], NT) * keep.astype(F32)).astype(BF16)


def add_terms(sums, x, past, cot, hidden, d_pre, fresh):
    for total, term in zip(sums, (dot(d_pre, x, TN), dot(d_pre, past, TN), dot(cot, hidden, TN))):
        if fresh:
            total[...] = term
        else:
            total[...] += term


def layer_rows(part, ins, out_ref, cur_ref, prior_ref, sums, fresh):
    x_ref, past_ref, keep_ref, cot_ref, conv_ref, res_ref = ins
    rows, back = pl.ds(*part), pl.ds(part[0] - FIRST, part[1])
    x, cot, keep = x_ref[rows, :], cot_ref[rows, :], widened(keep_ref[rows, :])
    past = past_ref[...] * keep
    hidden, d_pre = gates(x, past, cot, conv_ref, res_ref)
    results(rows, x, cot, hidden, d_pre, conv_ref, res_ref, out_ref, cur_ref)
    prior_ref[back, :] = past_grads(d_pre, keep, conv_ref)
    add_terms(sums, x, past, cot, hidden, d_pre, fresh)


def first_kernel(part, *refs):
    out, cur, prior, *sums = refs[6:]
    layer_rows(part, refs[:6], out, cur, prior, sums, True)


def next_kernel(part, *refs):
    out, cur, prior, *sums = refs[12:]
    layer_rows(part, refs[:6], out, cur, prior, sums, False)


def later_kernel(x_ref, theirs_ref, conv_ref, res_ref, *refs):
    *sums, later_ref = refs[3:]
    x, cot = theirs_ref[:FIRST, :], theirs_ref[FIRST : 2 * FIRST, :]
    wide = theirs_ref[2 * FIRST :, :]
    keep = widened(jnp.concatenate([wide[:, i : i + 128] for i in range(0, WIDTH, 128)], 0))
    past = x_ref[:FIRST, :] * keep
    hidden, d_pre = gates(x, past, cot, conv_ref, res_ref)
    later_ref[...] = past_grads(d_pre, keep, conv_ref)
    add_terms(sums, x, past, cot, hidden, d_pre, False)


def own_first_kernel(x_ref, past_ref, keep_ref, cot_ref, conv_ref, res_ref, _out, _cur, out_ref, cur_ref):
    rows = pl.ds(0, FIRST)
    x, cot = x_ref[rows, :], cot_ref[rows, :]
    past = past_ref[...] * widened(keep_ref[rows, :])
    hidden, d_pre = gates(x, past, cot, conv_ref, res_ref)
    results(rows, x, cot, hidden, d_pre, conv_ref, res_ref, out_ref, cur_ref)


def last_kernel(part, where, *refs):
    out, cur, prior, *sums, own, send = refs[12:]
    layer_rows(part, refs[:6], out, cur, prior, sums, False)
    acc0, acc1, accr = sums
    core = where[0]
    for side, table in ((1 - core, send), (core, own)):
        for p in range(2):
            for s in range(4 * NX):
                z, x_at = s // NX, s % NX
                row = (p * 4 + z) * NX + x_at
                at = pl.ds(pl.multiple_of(row * 32 + side * 16, 16), 16)
                now, past = acc0[at, :], acc1[at, :]
                for y in range(NY):
                    lanes = slice(y * 128, y * 128 + 128)
                    slot = (p, y, x_at)
                    table[slot + (slice(z * 16, z * 16 + 16),)] = now[:, lanes]
                    table[slot + (slice(64 + z * 16, 80 + z * 16),)] = past[:, lanes]
            for pair in range(2 * NX):
                z, x_at = pair // NX * 2, pair % NX
                halves = []
                for i in range(2):
                    row = (p * 4 + z + i) * NX + x_at
                    halves.append(accr[pl.ds(pl.multiple_of(row * 16 + side * 8, 8), 8), :])
                both = jnp.concatenate(halves, 0)
                for y in range(NY):
                    slot = (p, y, x_at)
                    table[slot + (slice(128 + z * 8, 144 + z * 8),)] = both[:, y * 128 : y * 128 + 128]


def layer(where, x, pasts, keep, cot, conv, res, theirs):
    rows = [((ROWS, WIDTH), BF16), ((ROWS, WIDTH), F32), ((ROWS - FIRST, WIDTH), BF16)]
    totals = [(BIG, F32), (BIG, F32), (SMALL, F32)]
    aliases = {6 + j: j for j in range(6)}
    ins = lambda i: [x, pasts[i], keep, cot, conv, res]
    kernel = lambda f, i: functools.partial(f, PARTS[i])
    *done, s0, s1, s2 = call(kernel(first_kernel, 0), "layer_first", ins(0), rows + totals, limit=16)
    *sums, later = call(
        later_kernel,
        "layer_later",
        [x, theirs, conv, res, s0, s1, s2],
        [*totals, ((FIRST, WIDTH), BF16)],
        aliases={4: 0, 5: 1, 6: 2},
        limit=16,
    )
    state = call(kernel(next_kernel, 1), "layer_next", [*ins(1), *done, *sums], rows + totals, aliases=aliases, limit=16)
    out, cur, prior, _, _, _, own, send = call(
        kernel(last_kernel, 2),
        "layer_last",
        [*ins(2), *state],
        [*rows, *totals, (TABLE, F32), (TABLE, F32)],
        where,
        aliases=aliases,
        limit=16,
    )
    return out, cur, prior, later, own, send


def after_core(where, own, got, *outs):
    y = where[1]
    for p, (near, far) in enumerate(((1, 3), (3, 1))):
        keep, send = outs[2 * p], outs[2 * p + 1]
        for i, (stay, leave) in enumerate(((0, near), (far, 2))):
            keep[i] = own[p, y ^ stay] + got[p, y ^ stay]
            send[i] = (own[p, y ^ leave] + got[p, y ^ leave]).astype(BF16)


def after_y(keep0, got0, keep1, got1, _past, own0, send0, own1, send1):
    for keep, got, own, send in ((keep0, got0, own0, send0), (keep1, got1, own1, send1)):
        own[...] = keep[0] + got[0].astype(F32)
        send[...] = (keep[1] + got[1].astype(F32)).astype(BF16)


def before_seq(own0, got0, own1, got1, *rest):
    blocks = rest[-1]
    for p, (own, got) in enumerate(((own0, got0), (own1, got1))):
        for x in range(NX):
            total = own[x] + got[x].astype(F32)
            for z in range(4):
                rows = (total[z * 16 : z * 16 + 16], total[64 + z * 16 : 80 + z * 16], total[128 + z * 8 : 136 + z * 8])
                blocks[(p * 4 + z) * NX + x] = jnp.concatenate(rows, 0).astype(BF16)


def after_seq(pieces, out):
    total = pieces[0].astype(F32)
    for i in range(1, NX * NZ):
        total = total + pieces[i].astype(F32)
    out[...] = total * (1.0 / 512.0)


def join(where, mine, got, both):
    both[where[0]] = mine[...]
    both[1 - where[0]] = got[...]


def assemble(where, *refs):
    conv, res, table = refs[4:]
    for j in range(4):
        table[j] = refs[j][...]
    for y in range(NY):
        pair = table[where[1] ^ y]
        lanes = slice(y * 128, y * 128 + 128)
        for c in range(NC):
            conv[0, c * 16 : c * 16 + 16, lanes] = pair[c, :16]
            conv[1, c * 16 : c * 16 + 16, lanes] = pair[c, 16:32]
            res[c * 8 : c * 8 + 8, lanes] = pair[c, 32:]


def reduce_terms(where, own, send, following, past_first, out):
    got = grp_swap(send, 1)
    pair, half = (2,) + HALF, HALF
    keep0, send0, keep1, send1 = call(after_core, "after_core", [own, got], [(pair, F32), (pair, BF16)] * 2, where)
    got0, got1 = y_swap(send0, 1), y_swap(send1, 3)
    own0, send0, own1, send1 = call(after_y, "after_y", [keep0, got0, keep1, got1, past_first], [(half, F32), (half, BF16)] * 2)
    got0, got1 = y_swap(send0, 3), y_swap(send1, 1)
    (blocks,) = call(before_seq, "before_seq", [own0, got0, own1, got1, following, out], [((NX * NZ,) + PIECE, BF16)], far=(5,))
    pieces = lax.all_to_all(blocks, "seq", 0, 0)
    (mine,) = call(after_seq, "after_seq", [pieces], [(PIECE, F32)])
    (both,) = call(join, "join", [mine, grp_swap(mine, 1)], [((2,) + PIECE, F32)], where)
    table = {0: both}
    for j in (2, 1, 3):
        table[j] = y_swap(both, j)
    conv, res = call(
        assemble,
        "assemble",
        [table[j] for j in range(4)],
        [((2, 32, WIDTH), F32), ((16, WIDTH), F32)],
        where,
        [pltpu.VMEM((4, 2) + PIECE, F32)],
        free_outs=True,
    )
    return conv.swapaxes(1, 2), res.T


def local(inputs, offsets, conv_weight, res_weight, cotangent):
    x, cot = inputs[0], cotangent[0]
    jump = DILATION_GAP // ROWS
    grp, seq = lax.axis_index("grp"), lax.axis_index("seq")
    where = jnp.stack([grp & 1, grp >> 1, seq & 3, seq >> 2]).astype(jnp.int32)
    keep = jnp.broadcast_to((offsets[0] >= DILATION_GAP).astype(BF16)[:, None], (ROWS, 128))
    *chunks, mine = split(keep, x, cot)
    pasts = [shifted(chunk, jump) for chunk in chunks]
    theirs = shifted(mine, -jump)
    out, cur, prior, later, own, send = layer(
        where, x, pasts, keep, cot, conv_weight, res_weight, theirs
    )
    following = shifted(prior, -jump)
    past_first = shifted(x[:FIRST], jump)
    out, cur = call(
        own_first_kernel,
        "layer_own_first",
        [x, past_first, keep, cot, conv_weight, res_weight, out, cur],
        [((ROWS, WIDTH), BF16), ((ROWS, WIDTH), F32)],
        aliases={6: 0, 7: 1},
        limit=16,
    )
    (out,) = call(flush, "flush", [out], [((ROWS, WIDTH), BF16)], scratch=[pltpu.SemaphoreType.DMA((1,))], far_outs=True)
    d_conv, d_res = reduce_terms(where, own, send, following, past_first, out)
    d_inputs = (cur + jnp.concatenate([later, following], 0).astype(F32)).astype(BF16)
    return (out[None], d_inputs[None], d_conv, d_res)


def solution(mesh):
    placed = (P("grp", "seq", None), P("grp", "seq"), P(), P(), P("grp", "seq", None))
    return jax.shard_map(
        local,
        mesh=mesh,
        in_specs=placed,
        out_specs=(
            P("grp", "seq", None),
            P("grp", "seq", None),
            P(None, None, "seq"),
            P(None, "seq"),
        ),
        check_vma=False,
    )
```

```python
import functools

import jax
import jax.numpy as jnp
from jax import lax
from jax.experimental import pallas as pl
from jax.experimental.pallas import tpu as pltpu
from jax.sharding import PartitionSpec as P

DILATION_GAP = 4096
F32 = jnp.float32
BF16 = jnp.bfloat16
NX, NY, NZ, NC = 4, 4, 8, 2
WIDTH = 512
ROWS = 1024
FIRST = 256
PARTS = ((256, 256), (512, 256), (768, 256))
TABLE = (2, 4, 4, 160, 128)
BIG, SMALL = (2 * WIDTH, WIDTH), (WIDTH, WIDTH)
HALF, PIECE = (4, 160, 128), (40, 128)
MIB = 1024 * 1024
LAYER = dict(limit=16, flops=4 << 30)

NN = ((1,), (0,))
NT = ((1,), (1,))
TN = ((0,), (0,))


def shifted(value, by):
    return lax.ppermute(value, "seq", [(i, (i + by) % (NX * NZ)) for i in range(NX * NZ)])


def grp_swap(value, j):
    return lax.ppermute(value, "grp", [(i, i ^ j) for i in range(NY * NC)])


def y_swap(value, j):
    return grp_swap(value, j * NC)


def call(kernel, name, args, outs, where=None, scratch=(), aliases=None, far=(), free_outs=False, far_outs=False, limit=2, flops=0):
    here, there = pl.BlockSpec(memory_space=pltpu.VMEM), pl.BlockSpec(memory_space=pltpu.HBM)
    lead = [] if where is None else [where]
    return pl.pallas_call(
        kernel,
        in_specs=[pl.BlockSpec(memory_space=pltpu.SMEM)] * len(lead)
        + [there if i in far else here for i in range(len(args))],
        out_specs=[there if far_outs else here] * len(outs),
        out_shape=[(pltpu.HBM if far_outs else jax.ShapeDtypeStruct if free_outs else pltpu.VMEM)(*out) for out in outs],
        scratch_shapes=list(scratch),
        input_output_aliases={len(lead) + i: o for i, o in (aliases or {}).items()},
        compiler_params=pltpu.CompilerParams(vmem_limit_bytes=limit * MIB),
        cost_estimate=pl.CostEstimate(flops=flops, bytes_accessed=flops // 1024, transcendentals=0) if flops else None,
        name=name,
    )(*lead, *[pltpu.with_memory_space_constraint(a, pltpu.HBM if i in far else pltpu.VMEM) for i, a in enumerate(args)])


def dot(a, b, contract):
    return lax.dot_general(a, b, (contract, ((), ())), preferred_element_type=F32)


def stage(pairs, sems):
    copies = [pltpu.make_async_copy(src, dst, sems.at[i]) for i, (src, dst) in enumerate(pairs)]
    for copy in copies:
        copy.start()
    for copy in copies:
        copy.wait()


def flush(out, far, sems):
    stage([(out, far)], sems)


def in_four(source, lo, count, result, at=0):
    step = count // 4
    return [(source.at[pl.ds(lo + i, step)], result.at[pl.ds(at + i, step)]) for i in range(0, count, step)]


def split_kernel(cuts, *refs):
    sems, pairs = refs[-1], []
    for source, lo, count, result, at in cuts:
        pairs += in_four(refs[source], lo, count, refs[result], at)
    stage(pairs, sems)


def split(name, sources, cuts, outs, near=()):
    count = len(sources) + len(near)
    cuts = [(source, lo, rows, count + result, at) for source, lo, rows, result, at in cuts]
    sems = [pltpu.SemaphoreType.DMA((4 * len(cuts),))]
    outs = [((rows, WIDTH), BF16) for rows in outs]
    return call(functools.partial(split_kernel, cuts), name, [*sources, *near], outs, far=range(len(sources)), scratch=sems)


def split_all(keep, x, cot):
    quarter = FIRST // 4
    wide = jnp.concatenate([keep[i : i + quarter] for i in range(0, FIRST, quarter)], 1)
    chunks = split("split_parts", [x], [(0, *part, i, 0) for i, part in enumerate(PARTS)], [count for _, count in PARTS])
    cuts = [(0, 0, FIRST, 0, 0), (1, 0, FIRST, 0, FIRST), (2, 0, quarter, 0, 2 * FIRST)]
    (mine,) = split("split_first", [x, cot], cuts, [2 * FIRST + quarter], [wide, chunks[0]])
    return chunks, mine


def gates(pre, cot, res_ref):
    filt = jnp.tanh(pre[:, :WIDTH])
    gate = jax.nn.sigmoid(pre[:, WIDTH:])
    hidden = (filt * gate).astype(BF16)
    d_hidden = dot(cot, res_ref[...], NT)
    d_filter = d_hidden * gate * (1.0 - filt * filt)
    d_gate = d_hidden * filt * gate * (1.0 - gate)
    return hidden, jnp.concatenate([d_filter.astype(BF16), d_gate.astype(BF16)], 1)


def widened(keep):
    return jnp.concatenate([keep] * (WIDTH // 128), 1)


def results(rows, x, cot, hidden, d_pre, conv_ref, res_ref, out_ref, cur_ref):
    out_ref[rows, :] = (x.astype(F32) + dot(hidden, res_ref[...], NN)).astype(BF16)
    cur_ref[rows, :] = cot.astype(F32) + dot(d_pre, conv_ref[0], NT)


def past_grads(d_pre, keep, conv_ref):
    return (dot(d_pre, conv_ref[1], NT) * keep.astype(F32)).astype(BF16)


def add_terms(sums, x, past, cot, hidden, d_pre, fresh):
    for total, term in zip(sums, (dot(d_pre, x, TN), dot(d_pre, past, TN), dot(cot, hidden, TN))):
        if fresh:
            total[...] = term
        else:
            total[...] += term


def layer_rows(part, loaded, past_ref, keep_ref, conv_ref, res_ref, out_ref, cur_ref, prior_ref, sums, fresh):
    rows, back = pl.ds(*part), pl.ds(part[0] - FIRST, part[1])
    x_of, cot_of = loaded(rows)
    keep = widened(keep_ref[rows, :])
    past = past_ref[...] * keep
    x = x_of()
    pre = dot(x, conv_ref[0], NN) + dot(past, conv_ref[1], NN)
    cot = cot_of()
    hidden, d_pre = gates(pre, cot, res_ref)
    results(rows, x, cot, hidden, d_pre, conv_ref, res_ref, out_ref, cur_ref)
    prior_ref[back, :] = past_grads(d_pre, keep, conv_ref)
    add_terms(sums, x, past, cot, hidden, d_pre, fresh)


def first_kernel(part, x_far, past, keep, cot_far, conv, res, out, cur, prior, *rest):
    *sums, x_near, cot_near, sems = rest

    def loaded(rows):
        ways = []
        for i, (far, near) in enumerate(((x_far, x_near), (cot_far, cot_near))):
            pairs = in_four(far, part[0], part[1], near)
            copies = [pltpu.make_async_copy(a, b, sems.at[4 * i + j]) for j, (a, b) in enumerate(pairs)]
            for copy in copies:
                copy.start()
            ways.append((copies, near))

        def arrived(copies, near):
            for copy in copies:
                copy.wait()
            return near[...]

        return [functools.partial(arrived, *way) for way in ways]

    layer_rows(part, loaded, past, keep, conv, res, out, cur, prior, sums, True)


def in_place(x_ref, cot_ref):
    return lambda rows: (lambda: x_ref[rows, :], lambda: cot_ref[rows, :])


def next_kernel(part, *refs):
    x, past, keep, cot, conv, res = refs[:6]
    out, cur, prior, *sums = refs[12:]
    layer_rows(part, in_place(x, cot), past, keep, conv, res, out, cur, prior, sums, False)


def later_kernel(x_ref, theirs_ref, conv_ref, res_ref, *refs):
    *sums, later_ref = refs[3:]
    x, cot = theirs_ref[:FIRST, :], theirs_ref[FIRST : 2 * FIRST, :]
    wide = theirs_ref[2 * FIRST :, :]
    keep = widened(jnp.concatenate([wide[:, i : i + 128] for i in range(0, WIDTH, 128)], 0))
    past = x_ref[:FIRST, :] * keep
    pre = dot(x, conv_ref[0], NN) + dot(past, conv_ref[1], NN)
    hidden, d_pre = gates(pre, cot, res_ref)
    later_ref[...] = past_grads(d_pre, keep, conv_ref)
    add_terms(sums, x, past, cot, hidden, d_pre, False)


def own_first_kernel(x_ref, past_ref, keep_ref, cot_ref, conv_ref, res_ref, _out, _cur, out_ref, cur_ref):
    rows = pl.ds(0, FIRST)
    x, cot = x_ref[rows, :], cot_ref[rows, :]
    past = past_ref[...] * widened(keep_ref[rows, :])
    pre = dot(x, conv_ref[0], NN) + dot(past, conv_ref[1], NN)
    hidden, d_pre = gates(pre, cot, res_ref)
    results(rows, x, cot, hidden, d_pre, conv_ref, res_ref, out_ref, cur_ref)


def last_kernel(part, where, *refs):
    x, past, keep, cot, conv, res = refs[:6]
    out, cur, prior, *sums, own, send = refs[12:]
    layer_rows(part, in_place(x, cot), past, keep, conv, res, out, cur, prior, sums, False)
    acc0, acc1, accr = sums
    core = where[0]
    for side, table in ((1 - core, send), (core, own)):
        for p in range(2):
            for s in range(4 * NX):
                z, x_at = s // NX, s % NX
                row = (p * 4 + z) * NX + x_at
                at = pl.ds(pl.multiple_of(row * 32 + side * 16, 16), 16)
                now, past = acc0[at, :], acc1[at, :]
                for y in range(NY):
                    lanes = slice(y * 128, y * 128 + 128)
                    slot = (p, y, x_at)
                    table[slot + (slice(z * 16, z * 16 + 16),)] = now[:, lanes]
                    table[slot + (slice(64 + z * 16, 80 + z * 16),)] = past[:, lanes]
            for pair in range(2 * NX):
                z, x_at = pair // NX * 2, pair % NX
                halves = []
                for i in range(2):
                    row = (p * 4 + z + i) * NX + x_at
                    halves.append(accr[pl.ds(pl.multiple_of(row * 16 + side * 8, 8), 8), :])
                both = jnp.concatenate(halves, 0)
                for y in range(NY):
                    slot = (p, y, x_at)
                    table[slot + (slice(128 + z * 8, 144 + z * 8),)] = both[:, y * 128 : y * 128 + 128]


def layer(where, x, pasts, keep, cot, conv, res, theirs):
    rows = [((ROWS, WIDTH), BF16), ((ROWS, WIDTH), F32), ((ROWS - FIRST, WIDTH), BF16)]
    totals = [(BIG, F32), (BIG, F32), (SMALL, F32)]
    aliases = {6 + j: j for j in range(6)}
    ins = lambda i: [x, pasts[i], keep, cot, conv, res]
    kernel = lambda f, i: functools.partial(f, PARTS[i])
    x_far, cot_far = x, cot
    count = PARTS[0][1]
    state = call(
        kernel(first_kernel, 0),
        "layer_first",
        [x_far, pasts[0], keep, cot_far, conv, res],
        rows + totals,
        far=(0, 3),
        scratch=[pltpu.VMEM((count, WIDTH), BF16), pltpu.VMEM((count, WIDTH), BF16), pltpu.SemaphoreType.DMA((8,))],
        **LAYER,
    )
    *done, s0, s1, s2 = call(kernel(next_kernel, 1), "layer_next", [*ins(1), *state], rows + totals, aliases=aliases, **LAYER)
    *sums, later = call(
        later_kernel,
        "layer_later",
        [x, theirs, conv, res, s0, s1, s2],
        [*totals, ((FIRST, WIDTH), BF16)],
        aliases={4: 0, 5: 1, 6: 2},
        **LAYER,
    )
    out, cur, prior, _, _, _, own, send = call(
        kernel(last_kernel, 2),
        "layer_last",
        [*ins(2), *done, *sums],
        [*rows, *totals, (TABLE, F32), (TABLE, F32)],
        where,
        aliases=aliases,
        **LAYER,
    )
    return out, cur, prior, later, own, send


def after_core(where, own, got, *outs):
    y = where[1]
    for p, (near, far) in enumerate(((1, 3), (3, 1))):
        keep, send = outs[2 * p], outs[2 * p + 1]
        for i, (stay, leave) in enumerate(((0, near), (far, 2))):
            keep[i] = own[p, y ^ stay] + got[p, y ^ stay]
            send[i] = (own[p, y ^ leave] + got[p, y ^ leave]).astype(BF16)


def after_y(keep0, got0, keep1, got1, _past, own0, send0, own1, send1):
    for keep, got, own, send in ((keep0, got0, own0, send0), (keep1, got1, own1, send1)):
        own[...] = keep[0] + got[0].astype(F32)
        send[...] = (keep[1] + got[1].astype(F32)).astype(BF16)


def before_seq(own0, got0, own1, got1, *rest):
    blocks = rest[-1]
    for p, (own, got) in enumerate(((own0, got0), (own1, got1))):
        for x in range(NX):
            total = own[x] + got[x].astype(F32)
            for z in range(4):
                rows = (total[z * 16 : z * 16 + 16], total[64 + z * 16 : 80 + z * 16], total[128 + z * 8 : 136 + z * 8])
                blocks[(p * 4 + z) * NX + x] = jnp.concatenate(rows, 0).astype(BF16)


def after_seq(pieces, out):
    total = pieces[0].astype(F32)
    for i in range(1, NX * NZ):
        total = total + pieces[i].astype(F32)
    out[...] = total * (1.0 / 512.0)


def join(where, mine, got, both):
    both[where[0]] = mine[...]
    both[1 - where[0]] = got[...]


def assemble(where, *refs):
    conv, res, table = refs[4:]
    for j in range(4):
        table[j] = refs[j][...]
    for y in range(NY):
        pair = table[where[1] ^ y]
        lanes = slice(y * 128, y * 128 + 128)
        for c in range(NC):
            conv[0, c * 16 : c * 16 + 16, lanes] = pair[c, :16]
            conv[1, c * 16 : c * 16 + 16, lanes] = pair[c, 16:32]
            res[c * 8 : c * 8 + 8, lanes] = pair[c, 32:]


def reduce_terms(where, own, send, following, past_first, out):
    got = grp_swap(send, 1)
    pair, half = (2,) + HALF, HALF
    keep0, send0, keep1, send1 = call(after_core, "after_core", [own, got], [(pair, F32), (pair, BF16)] * 2, where)
    got0, got1 = y_swap(send0, 1), y_swap(send1, 3)
    own0, send0, own1, send1 = call(after_y, "after_y", [keep0, got0, keep1, got1, past_first], [(half, F32), (half, BF16)] * 2)
    got0, got1 = y_swap(send0, 3), y_swap(send1, 1)
    (blocks,) = call(before_seq, "before_seq", [own0, got0, own1, got1, following, out], [((NX * NZ,) + PIECE, BF16)], far=(5,))
    pieces = lax.all_to_all(blocks, "seq", 0, 0)
    (mine,) = call(after_seq, "after_seq", [pieces], [(PIECE, F32)])
    (both,) = call(join, "join", [mine, grp_swap(mine, 1)], [((2,) + PIECE, F32)], where)
    table = {0: both}
    for j in (2, 1, 3):
        table[j] = y_swap(both, j)
    conv, res = call(
        assemble,
        "assemble",
        [table[j] for j in range(4)],
        [((2, 32, WIDTH), F32), ((16, WIDTH), F32)],
        where,
        [pltpu.VMEM((4, 2) + PIECE, F32)],
        free_outs=True,
    )
    return conv.swapaxes(1, 2), res.T


def local(inputs, offsets, conv_weight, res_weight, cotangent):
    x, cot = inputs[0], cotangent[0]
    jump = DILATION_GAP // ROWS
    grp, seq = lax.axis_index("grp"), lax.axis_index("seq")
    where = jnp.stack([grp & 1, grp >> 1, seq & 3, seq >> 2]).astype(jnp.int32)
    keep = jnp.broadcast_to((offsets[0] >= DILATION_GAP).astype(BF16)[:, None], (ROWS, 128))
    chunks, mine = split_all(keep, x, cot)
    pasts = [shifted(chunk, jump) for chunk in chunks]
    theirs = shifted(mine, -jump)
    out, cur, prior, later, own, send = layer(
        where, x, pasts, keep, cot, conv_weight, res_weight, theirs
    )
    following = shifted(prior, -jump)
    past_first = shifted(x[:FIRST], jump)
    out, cur = call(
        own_first_kernel,
        "layer_own_first",
        [x, past_first, keep, cot, conv_weight, res_weight, out, cur],
        [((ROWS, WIDTH), BF16), ((ROWS, WIDTH), F32)],
        aliases={6: 0, 7: 1},
        **LAYER,
    )
    (out,) = call(flush, "flush", [out], [((ROWS, WIDTH), BF16)], scratch=[pltpu.SemaphoreType.DMA((1,))], far_outs=True)
    d_conv, d_res = reduce_terms(where, own, send, following, past_first, out)
    d_inputs = (cur + jnp.concatenate([later, following], 0).astype(F32)).astype(BF16)
    return (out[None], d_inputs[None], d_conv, d_res)


def solution(mesh):
    placed = (P("grp", "seq", None), P("grp", "seq"), P(), P(), P("grp", "seq", None))
    return jax.shard_map(
        local,
        mesh=mesh,
        in_specs=placed,
        out_specs=(
            P("grp", "seq", None),
            P("grp", "seq", None),
            P(None, None, "seq"),
            P(None, "seq"),
        ),
        check_vma=False,
    )
```

```python
import functools

import jax
import jax.numpy as jnp
from jax import lax
from jax.experimental import pallas as pl
from jax.experimental.pallas import tpu as pltpu
from jax.sharding import PartitionSpec as P

DILATION_GAP = 4096
F32 = jnp.float32
BF16 = jnp.bfloat16
NX, NY, NZ, NC = 4, 4, 8, 2
WIDTH = 512
ROWS = 1024
FIRST = 256
PARTS = ((256, 256), (512, 256), (768, 256))
TABLE = (4, 4, 160, 128)
BIG, SMALL = (2 * WIDTH, WIDTH), (WIDTH, WIDTH)
HALF, PIECE = (4, 160, 128), (40, 128)
MIB = 1024 * 1024
LAYER = dict(limit=16, flops=4 << 30)

NN = ((1,), (0,))
NT = ((1,), (1,))
TN = ((0,), (0,))


def shifted(value, by):
    return lax.ppermute(value, "seq", [(i, (i + by) % (NX * NZ)) for i in range(NX * NZ)])


def grp_swap(value, j):
    return lax.ppermute(value, "grp", [(i, i ^ j) for i in range(NY * NC)])


def y_swap(value, j):
    return grp_swap(value, j * NC)


def call(kernel, name, args, outs, where=None, scratch=(), aliases=None, far=(), loose=(), free_outs=False, far_outs=False, limit=2, flops=0):
    here, there = pl.BlockSpec(memory_space=pltpu.VMEM), pl.BlockSpec(memory_space=pltpu.HBM)
    anywhere, lead = pl.BlockSpec(memory_space=pl.ANY), [] if where is None else [where]
    return pl.pallas_call(
        kernel,
        in_specs=[pl.BlockSpec(memory_space=pltpu.SMEM)] * len(lead)
        + [anywhere if i in loose else there if i in far else here for i in range(len(args))],
        out_specs=[there if far_outs else here] * len(outs),
        out_shape=[(pltpu.HBM if far_outs else jax.ShapeDtypeStruct if free_outs else pltpu.VMEM)(*out) for out in outs],
        scratch_shapes=list(scratch),
        input_output_aliases={len(lead) + i: o for i, o in (aliases or {}).items()},
        compiler_params=pltpu.CompilerParams(vmem_limit_bytes=limit * MIB),
        cost_estimate=pl.CostEstimate(flops=flops, bytes_accessed=flops // 1024, transcendentals=0) if flops else None,
        name=name,
    )(*lead, *[a if i in loose else pltpu.with_memory_space_constraint(a, pltpu.HBM if i in far else pltpu.VMEM) for i, a in enumerate(args)])


def dot(a, b, contract):
    return lax.dot_general(a, b, (contract, ((), ())), preferred_element_type=F32)


def stage(pairs, sems):
    copies = [pltpu.make_async_copy(src, dst, sems.at[i]) for i, (src, dst) in enumerate(pairs)]
    for copy in copies:
        copy.start()
    for copy in copies:
        copy.wait()


def flush(out, far, sems):
    stage([(out, far)], sems)


def in_four(source, lo, count, result, at=0):
    step = count // 4
    return [(source.at[pl.ds(lo + i, step)], result.at[pl.ds(at + i, step)]) for i in range(0, count, step)]


def split_kernel(cuts, *refs):
    sems, pairs = refs[-1], []
    for source, lo, count, result, at in cuts:
        pairs += in_four(refs[source], lo, count, refs[result], at)
    stage(pairs, sems)


def split(name, sources, cuts, outs, near=()):
    count = len(sources) + len(near)
    cuts = [(source, lo, rows, count + result, at) for source, lo, rows, result, at in cuts]
    sems = [pltpu.SemaphoreType.DMA((4 * len(cuts),))]
    outs = [((rows, WIDTH), BF16) for rows in outs]
    return call(functools.partial(split_kernel, cuts), name, [*sources, *near], outs, far=range(len(sources)), scratch=sems)


def split_all(keep, x, cot):
    quarter = FIRST // 4
    wide = jnp.concatenate([keep[i : i + quarter] for i in range(0, FIRST, quarter)], 1)
    counts = [count for _, count in PARTS]
    chunks = split("split_parts", [x], [(0, *part, i, 0) for i, part in enumerate(PARTS)], counts)
    cuts = [(0, 0, FIRST, 0, 0), (1, 0, FIRST, 0, FIRST), (2, 0, quarter, 0, 2 * FIRST)]
    (mine,) = split("split_first", [x, cot], cuts, [2 * FIRST + quarter], [wide, chunks[0]])
    return chunks, mine


def gates(pre, cot, res):
    filt = jnp.tanh(pre[:, :WIDTH])
    gate = jax.nn.sigmoid(pre[:, WIDTH:])
    hidden = (filt * gate).astype(BF16)
    d_hidden = dot(cot, res, NT)
    d_filter = d_hidden * gate * (1.0 - filt * filt)
    d_gate = d_hidden * filt * gate * (1.0 - gate)
    return hidden, jnp.concatenate([d_filter.astype(BF16), d_gate.astype(BF16)], 1)


def widened(keep):
    return jnp.concatenate([keep] * (WIDTH // 128), 1)


def results(rows, x, cot, hidden, d_pre, conv_ref, res, out_ref, cur_ref):
    out_ref[rows, :] = (x.astype(F32) + dot(hidden, res, NN)).astype(BF16)
    cur_ref[rows, :] = cot.astype(F32) + dot(d_pre, conv_ref[0], NT)


def past_grads(d_pre, keep, conv_ref):
    return (dot(d_pre, conv_ref[1], NT) * keep.astype(F32)).astype(BF16)


def add_terms(sums, x, past, cot, hidden, d_pre, fresh):
    for total, term in zip(sums, (dot(d_pre, x, TN), dot(d_pre, past, TN), dot(cot, hidden, TN))):
        if fresh:
            total[...] = term
        else:
            total[...] += term


class Fetch:
    def __init__(self, source, lo, count, near, sems, first=0):
        pairs = in_four(source, lo, count, near)
        self.near = near
        self.copies = [pltpu.make_async_copy(a, b, sems.at[first + i]) for i, (a, b) in enumerate(pairs)]
        for copy in self.copies:
            copy.start()

    def __call__(self):
        for copy in self.copies:
            copy.wait()
        return self.near[...]


def layer_rows(part, x_of, past_of, cot_of, res_of, keep_ref, conv_ref, out_ref, cur_ref, prior_ref, sums, fresh):
    rows, back = pl.ds(*part), pl.ds(part[0] - FIRST, part[1])
    keep = widened(keep_ref[rows, :])
    x = x_of()
    now = dot(x, conv_ref[0], NN)
    past = past_of() * keep
    pre = now + dot(past, conv_ref[1], NN)
    cot, res = cot_of(), res_of()
    hidden, d_pre = gates(pre, cot, res)
    results(rows, x, cot, hidden, d_pre, conv_ref, res, out_ref, cur_ref)
    prior_ref[back, :] = past_grads(d_pre, keep, conv_ref)
    add_terms(sums, x, past, cot, hidden, d_pre, fresh)


def first_kernel(part, x_far, past_far, keep, cot_far, conv, res_far, out, cur, prior, *rest):
    *sums, x, past, cot, res, sems = rest
    x_of = Fetch(x_far, *part, x, sems)
    past_of = Fetch(past_far, 0, part[1], past, sems, 4)
    cot_of = Fetch(cot_far, *part, cot, sems, 8)
    res_of = Fetch(res_far, 0, WIDTH, res, sems, 12)
    layer_rows(part, x_of, past_of, cot_of, res_of, keep, conv, out, cur, prior, sums, True)


def in_place(part, refs, out, cur, prior, sums):
    x, past, keep, cot, conv, res = refs
    rows = pl.ds(*part)
    ways = (lambda: x[rows, :], lambda: past[...], lambda: cot[rows, :], lambda: res[...])
    layer_rows(part, *ways, keep, conv, out, cur, prior, sums, False)


def next_kernel(part, *refs):
    out, cur, prior, *sums = refs[12:]
    in_place(part, refs[:6], out, cur, prior, sums)


def later_kernel(x_ref, theirs_ref, conv_ref, res_ref, *refs):
    *sums, later_ref = refs[3:]
    x, cot = theirs_ref[:FIRST, :], theirs_ref[FIRST : 2 * FIRST, :]
    wide = theirs_ref[2 * FIRST :, :]
    keep = widened(jnp.concatenate([wide[:, i : i + 128] for i in range(0, WIDTH, 128)], 0))
    past = x_ref[:FIRST, :] * keep
    pre = dot(x, conv_ref[0], NN) + dot(past, conv_ref[1], NN)
    hidden, d_pre = gates(pre, cot, res_ref[...])
    later_ref[...] = past_grads(d_pre, keep, conv_ref)
    add_terms(sums, x, past, cot, hidden, d_pre, False)


def own_first_kernel(x_ref, past_ref, keep_ref, cot_ref, conv_ref, res_ref, _out, _cur, out_ref, cur_ref):
    rows = pl.ds(0, FIRST)
    x, cot = x_ref[rows, :], cot_ref[rows, :]
    past = past_ref[...] * widened(keep_ref[rows, :])
    pre = dot(x, conv_ref[0], NN) + dot(past, conv_ref[1], NN)
    hidden, d_pre = gates(pre, cot, res_ref[...])
    results(rows, x, cot, hidden, d_pre, conv_ref, res_ref[...], out_ref, cur_ref)


def last_kernel(part, where, *refs):
    out, cur, prior, *sums, own0, own1, send0, send1 = refs[12:]
    in_place(part, refs[:6], out, cur, prior, sums)
    acc0, acc1, accr = sums
    core = where[0]
    for side, tables in ((1 - core, (send0, send1)), (core, (own0, own1))):
        for p, table in enumerate(tables):
            for s in range(4 * NX):
                z, x_at = s // NX, s % NX
                row = (p * 4 + z) * NX + x_at
                at = pl.ds(pl.multiple_of(row * 32 + side * 16, 16), 16)
                now, past = acc0[at, :], acc1[at, :]
                for y in range(NY):
                    lanes = slice(y * 128, y * 128 + 128)
                    slot = (y, x_at)
                    table[slot + (slice(z * 16, z * 16 + 16),)] = now[:, lanes]
                    table[slot + (slice(64 + z * 16, 80 + z * 16),)] = past[:, lanes]
            for pair in range(2 * NX):
                z, x_at = pair // NX * 2, pair % NX
                halves = []
                for i in range(2):
                    row = (p * 4 + z + i) * NX + x_at
                    halves.append(accr[pl.ds(pl.multiple_of(row * 16 + side * 8, 8), 8), :])
                both = jnp.concatenate(halves, 0)
                for y in range(NY):
                    slot = (y, x_at)
                    table[slot + (slice(128 + z * 8, 144 + z * 8),)] = both[:, y * 128 : y * 128 + 128]


def layer(where, x, pasts, keep, cot, conv, res, theirs):
    rows = [((ROWS, WIDTH), BF16), ((ROWS, WIDTH), F32), ((ROWS - FIRST, WIDTH), BF16)]
    totals = [(BIG, F32), (BIG, F32), (SMALL, F32)]
    aliases = {6 + j: j for j in range(6)}
    ins = lambda i: [x, pasts[i], keep, cot, conv, res]
    kernel = lambda f, i: functools.partial(f, PARTS[i])
    x_far, cot_far = x, cot
    carry = dict(aliases=aliases, **LAYER)
    count = PARTS[0][1]
    state = call(
        kernel(first_kernel, 0),
        "layer_first",
        [x_far, pasts[0], keep, cot_far, conv, res],
        rows + totals,
        far=(0, 3, 5),
        loose=(1,),
        scratch=[pltpu.VMEM((count, WIDTH), BF16)] * 3 + [pltpu.VMEM((WIDTH, WIDTH), BF16), pltpu.SemaphoreType.DMA((16,))],
        **LAYER,
    )
    *done, s0, s1, s2 = call(kernel(next_kernel, 1), "layer_next", [*ins(1), *state], rows + totals, **carry)
    *sums, later = call(
        later_kernel,
        "layer_later",
        [x, theirs, conv, res, s0, s1, s2],
        [*totals, ((FIRST, WIDTH), BF16)],
        aliases={4: 0, 5: 1, 6: 2},
        **LAYER,
    )
    out, cur, prior, _, _, _, own0, own1, send0, send1 = call(
        kernel(last_kernel, 2),
        "layer_last",
        [*ins(2), *done, *sums],
        [*rows, *totals, *[(TABLE, F32)] * 4],
        where,
        **carry,
    )
    return out, cur, prior, later, (own0, own1), (send0, send1)


def after_core(near, where, own, got, keep, send):
    y = where[1]
    for i, (stay, leave) in enumerate(((0, near), (4 - near, 2))):
        keep[i] = own[y ^ stay] + got[y ^ stay]
        send[i] = (own[y ^ leave] + got[y ^ leave]).astype(BF16)


def after_y(keep, got, own, send):
    own[...] = keep[0] + got[0].astype(F32)
    send[...] = (keep[1] + got[1].astype(F32)).astype(BF16)


def before_seq(own0, got0, own1, got1, *rest):
    blocks = rest[-1]
    for p, (own, got) in enumerate(((own0, got0), (own1, got1))):
        for x in range(NX):
            total = own[x] + got[x].astype(F32)
            for z in range(4):
                rows = (total[z * 16 : z * 16 + 16], total[64 + z * 16 : 80 + z * 16], total[128 + z * 8 : 136 + z * 8])
                blocks[(p * 4 + z) * NX + x] = jnp.concatenate(rows, 0).astype(BF16)


def after_seq(pieces, out):
    total = pieces[0].astype(F32)
    for i in range(1, NX * NZ):
        total = total + pieces[i].astype(F32)
    out[...] = total * (1.0 / 512.0)


def join(where, mine, got, both):
    both[where[0]] = mine[...]
    both[1 - where[0]] = got[...]


def assemble(where, *refs):
    conv, res, table = refs[4:]
    for j in range(4):
        table[j] = refs[j][...]
    for y in range(NY):
        pair = table[where[1] ^ y]
        lanes = slice(y * 128, y * 128 + 128)
        for c in range(NC):
            conv[0, c * 16 : c * 16 + 16, lanes] = pair[c, :16]
            conv[1, c * 16 : c * 16 + 16, lanes] = pair[c, 16:32]
            res[c * 8 : c * 8 + 8, lanes] = pair[c, 32:]


def reduce_terms(where, own, send, following, out):
    pair, half = (2,) + HALF, HALF
    got = [grp_swap(table, 1) for table in send]
    keep, own_y, got_y = [], [], []
    for p, near in enumerate((1, 3)):
        kernel = functools.partial(after_core, near)
        kept, leaving = call(kernel, "after_core", [own[p], got[p]], [(pair, F32), (pair, BF16)], where)
        keep.append(kept)
        got_y.append(y_swap(leaving, near))
    for p, far in enumerate((3, 1)):
        mine, leaving = call(after_y, "after_y", [keep[p], got_y[p]], [(half, F32), (half, BF16)])
        own_y += [mine, y_swap(leaving, far)]
    (blocks,) = call(before_seq, "before_seq", [*own_y, following, out], [((NX * NZ,) + PIECE, BF16)], far=(5,))
    pieces = lax.all_to_all(blocks, "seq", 0, 0)
    (mine,) = call(after_seq, "after_seq", [pieces], [(PIECE, F32)])
    (both,) = call(join, "join", [mine, grp_swap(mine, 1)], [((2,) + PIECE, F32)], where)
    table = {0: both}
    for j in (2, 1, 3):
        table[j] = y_swap(both, j)
    conv, res = call(
        assemble,
        "assemble",
        [table[j] for j in range(4)],
        [((2, 32, WIDTH), F32), ((16, WIDTH), F32)],
        where,
        [pltpu.VMEM((4, 2) + PIECE, F32)],
        free_outs=True,
    )
    return conv.swapaxes(1, 2), res.T


def local(inputs, offsets, conv_weight, res_weight, cotangent):
    x, cot = inputs[0], cotangent[0]
    jump = DILATION_GAP // ROWS
    grp, seq = lax.axis_index("grp"), lax.axis_index("seq")
    where = jnp.stack([grp & 1, grp >> 1, seq & 3, seq >> 2]).astype(jnp.int32)
    keep = jnp.broadcast_to((offsets[0] >= DILATION_GAP).astype(BF16)[:, None], (ROWS, 128))
    chunks, mine = split_all(keep, x, cot)
    pasts = [shifted(chunk, jump) for chunk in chunks]
    theirs = shifted(mine, -jump)
    out, cur, prior, later, own, send = layer(
        where, x, pasts, keep, cot, conv_weight, res_weight, theirs
    )
    following = shifted(prior, -jump)
    past_first = shifted(x[:FIRST], jump)
    out, cur = call(
        own_first_kernel,
        "layer_own_first",
        [x, past_first, keep, cot, conv_weight, res_weight, out, cur],
        [((ROWS, WIDTH), BF16), ((ROWS, WIDTH), F32)],
        aliases={6: 0, 7: 1},
        **LAYER,
    )
    (out,) = call(flush, "flush", [out], [((ROWS, WIDTH), BF16)], scratch=[pltpu.SemaphoreType.DMA((1,))], far_outs=True)
    d_conv, d_res = reduce_terms(where, own, send, following, out)
    d_inputs = (cur + jnp.concatenate([later, following], 0).astype(F32)).astype(BF16)
    return (out[None], d_inputs[None], d_conv, d_res)


def solution(mesh):
    placed = (P("grp", "seq", None), P("grp", "seq"), P(), P(), P("grp", "seq", None))
    return jax.shard_map(
        local,
        mesh=mesh,
        in_specs=placed,
        out_specs=(
            P("grp", "seq", None),
            P("grp", "seq", None),
            P(None, None, "seq"),
            P(None, "seq"),
        ),
        check_vma=False,
    )
```

```python
import functools

import jax
import jax.numpy as jnp
from jax import lax
from jax.experimental import pallas as pl
from jax.experimental.pallas import tpu as pltpu
from jax.sharding import PartitionSpec as P

DILATION_GAP = 4096
F32 = jnp.float32
BF16 = jnp.bfloat16
NX, NY, NZ, NC = 4, 4, 8, 2
WIDTH = 512
ROWS = 1024
FIRST = 256
PARTS = ((256, 256), (512, 256), (768, 256))
TABLE = (4, 4, 160, 128)
BIG, SMALL = (2 * WIDTH, WIDTH), (WIDTH, WIDTH)
HALF, PIECE = (4, 160, 128), (40, 128)
MIB = 1024 * 1024
LAYER = dict(limit=16, flops=4 << 30)

NN = ((1,), (0,))
NT = ((1,), (1,))
TN = ((0,), (0,))


def shifted(value, by):
    return lax.ppermute(value, "seq", [(i, (i + by) % (NX * NZ)) for i in range(NX * NZ)])


def grp_swap(value, j):
    return lax.ppermute(value, "grp", [(i, i ^ j) for i in range(NY * NC)])


def y_swap(value, j):
    return grp_swap(value, j * NC)


def call(kernel, name, args, outs, where=None, scratch=(), aliases=None, far=(), loose=(), free_outs=False, far_outs=False, limit=2, flops=0):
    here, there = pl.BlockSpec(memory_space=pltpu.VMEM), pl.BlockSpec(memory_space=pltpu.HBM)
    anywhere, lead = pl.BlockSpec(memory_space=pl.ANY), [] if where is None else [where]
    return pl.pallas_call(
        kernel,
        in_specs=[pl.BlockSpec(memory_space=pltpu.SMEM)] * len(lead)
        + [anywhere if i in loose else there if i in far else here for i in range(len(args))],
        out_specs=[there if far_outs else here] * len(outs),
        out_shape=[(pltpu.HBM if far_outs else jax.ShapeDtypeStruct if free_outs else pltpu.VMEM)(*out) for out in outs],
        scratch_shapes=list(scratch),
        input_output_aliases={len(lead) + i: o for i, o in (aliases or {}).items()},
        compiler_params=pltpu.CompilerParams(vmem_limit_bytes=limit * MIB),
        cost_estimate=pl.CostEstimate(flops=flops, bytes_accessed=flops // 1024, transcendentals=0) if flops else None,
        name=name,
    )(*lead, *[a if i in loose else pltpu.with_memory_space_constraint(a, pltpu.HBM if i in far else pltpu.VMEM) for i, a in enumerate(args)])


def dot(a, b, contract):
    return lax.dot_general(a, b, (contract, ((), ())), preferred_element_type=F32)


def stage(pairs, sems):
    copies = [pltpu.make_async_copy(src, dst, sems.at[i]) for i, (src, dst) in enumerate(pairs)]
    for copy in copies:
        copy.start()
    for copy in copies:
        copy.wait()


def flush(out, far, sems):
    stage([(out, far)], sems)


def in_four(source, lo, count, result, at=0):
    step = count // 4
    return [(source.at[pl.ds(lo + i, step)], result.at[pl.ds(at + i, step)]) for i in range(0, count, step)]


def split_kernel(cuts, *refs):
    sems, pairs = refs[-1], []
    for source, lo, count, result, at in cuts:
        pairs += in_four(refs[source], lo, count, refs[result], at)
    stage(pairs, sems)


def split(name, sources, cuts, outs, near=()):
    count = len(sources) + len(near)
    cuts = [(source, lo, rows, count + result, at) for source, lo, rows, result, at in cuts]
    sems = [pltpu.SemaphoreType.DMA((4 * len(cuts),))]
    outs = [((rows, WIDTH), BF16) for rows in outs]
    return call(functools.partial(split_kernel, cuts), name, [*sources, *near], outs, far=range(len(sources)), scratch=sems)


def split_all(keep, x, cot):
    quarter = FIRST // 4
    wide = jnp.concatenate([keep[i : i + quarter] for i in range(0, FIRST, quarter)], 1)
    counts = [count for _, count in PARTS]
    chunks = split("split_parts", [x], [(0, *part, i, 0) for i, part in enumerate(PARTS)], counts)
    cuts = [(0, 0, FIRST, 0, 0), (1, 0, FIRST, 0, FIRST), (2, 0, quarter, 0, 2 * FIRST)]
    (mine,) = split("split_first", [x, cot], cuts, [2 * FIRST + quarter], [wide, chunks[0]])
    return chunks, mine


def gates(pre, cot, res):
    filt = jnp.tanh(pre[:, :WIDTH])
    gate = jax.nn.sigmoid(pre[:, WIDTH:])
    hidden = (filt * gate).astype(BF16)
    d_hidden = dot(cot, res, NT)
    d_filter = d_hidden * gate * (1.0 - filt * filt)
    d_gate = d_hidden * filt * gate * (1.0 - gate)
    return hidden, jnp.concatenate([d_filter.astype(BF16), d_gate.astype(BF16)], 1)


def widened(keep):
    return jnp.concatenate([keep] * (WIDTH // 128), 1)


def results(rows, x, cot, hidden, d_pre, conv_ref, res, out_ref, cur_ref):
    out_ref[rows, :] = (x.astype(F32) + dot(hidden, res, NN)).astype(BF16)
    cur_ref[rows, :] = cot.astype(F32) + dot(d_pre, conv_ref[0], NT)


def past_grads(d_pre, keep, conv_ref):
    return (dot(d_pre, conv_ref[1], NT) * keep.astype(F32)).astype(BF16)


def add_terms(sums, x, past, cot, hidden, d_pre, fresh):
    for total, term in zip(sums, (dot(d_pre, x, TN), dot(d_pre, past, TN), dot(cot, hidden, TN))):
        if fresh:
            total[...] = term
        else:
            total[...] += term


class Fetch:
    def __init__(self, source, lo, count, near, sems, first=0):
        pairs = in_four(source, lo, count, near)
        self.near = near
        self.copies = [pltpu.make_async_copy(a, b, sems.at[first + i]) for i, (a, b) in enumerate(pairs)]
        for copy in self.copies:
            copy.start()

    def __call__(self):
        for copy in self.copies:
            copy.wait()
        return self.near[...]


def layer_rows(part, x_of, past_of, cot_of, res_of, keep_ref, conv_ref, out_ref, cur_ref, prior_ref, sums, fresh):
    rows, back = pl.ds(*part), pl.ds(part[0] - FIRST, part[1])
    keep = widened(keep_ref[rows, :])
    x = x_of()
    now = dot(x, conv_ref[0], NN)
    past = past_of() * keep
    pre = now + dot(past, conv_ref[1], NN)
    cot, res = cot_of(), res_of()
    hidden, d_pre = gates(pre, cot, res)
    results(rows, x, cot, hidden, d_pre, conv_ref, res, out_ref, cur_ref)
    prior_ref[back, :] = past_grads(d_pre, keep, conv_ref)
    add_terms(sums, x, past, cot, hidden, d_pre, fresh)


def first_kernel(part, x_far, past_far, keep, cot_far, conv, res_far, out, cur, prior, *rest):
    *sums, x, past, cot, res, sems = rest
    x_of = Fetch(x_far, *part, x, sems)
    past_of = Fetch(past_far, 0, part[1], past, sems, 4)
    cot_of = Fetch(cot_far, *part, cot, sems, 8)
    res_of = Fetch(res_far, 0, WIDTH, res, sems, 12)
    layer_rows(part, x_of, past_of, cot_of, res_of, keep, conv, out, cur, prior, sums, True)


def in_place(part, refs, out, cur, prior, sums):
    x, past, keep, cot, conv, res = refs
    rows = pl.ds(*part)
    ways = (lambda: x[rows, :], lambda: past[...], lambda: cot[rows, :], lambda: res[...])
    layer_rows(part, *ways, keep, conv, out, cur, prior, sums, False)


def next_kernel(part, *refs):
    out, cur, prior, *sums = refs[12:]
    in_place(part, refs[:6], out, cur, prior, sums)


def later_kernel(x_ref, theirs_ref, conv_ref, res_ref, *refs):
    *sums, later_ref = refs[3:]
    x, cot = theirs_ref[:FIRST, :], theirs_ref[FIRST : 2 * FIRST, :]
    wide = theirs_ref[2 * FIRST :, :]
    keep = widened(jnp.concatenate([wide[:, i : i + 128] for i in range(0, WIDTH, 128)], 0))
    past = x_ref[:FIRST, :] * keep
    pre = dot(x, conv_ref[0], NN) + dot(past, conv_ref[1], NN)
    hidden, d_pre = gates(pre, cot, res_ref[...])
    later_ref[...] = past_grads(d_pre, keep, conv_ref)
    add_terms(sums, x, past, cot, hidden, d_pre, False)


def own_first_kernel(x_ref, past_ref, keep_ref, cot_ref, conv_ref, res_ref, _out, _cur, out_ref, cur_ref):
    rows = pl.ds(0, FIRST)
    x, cot = x_ref[rows, :], cot_ref[rows, :]
    past = past_ref[...] * widened(keep_ref[rows, :])
    pre = dot(x, conv_ref[0], NN) + dot(past, conv_ref[1], NN)
    hidden, d_pre = gates(pre, cot, res_ref[...])
    results(rows, x, cot, hidden, d_pre, conv_ref, res_ref[...], out_ref, cur_ref)


def last_kernel(part, where, *refs):
    out, cur, prior, *sums, own0, own1, send0, send1 = refs[12:]
    in_place(part, refs[:6], out, cur, prior, sums)
    acc0, acc1, accr = sums
    core = where[0]
    for side, tables in ((1 - core, (send0, send1)), (core, (own0, own1))):
        for p, table in enumerate(tables):
            for s in range(4 * NX):
                z, x_at = s // NX, s % NX
                row = (p * 4 + z) * NX + x_at
                at = pl.ds(pl.multiple_of(row * 32 + side * 16, 16), 16)
                now, past = acc0[at, :], acc1[at, :]
                for y in range(NY):
                    lanes = slice(y * 128, y * 128 + 128)
                    slot = (y, x_at)
                    table[slot + (slice(z * 16, z * 16 + 16),)] = now[:, lanes]
                    table[slot + (slice(64 + z * 16, 80 + z * 16),)] = past[:, lanes]
            for pair in range(2 * NX):
                z, x_at = pair // NX * 2, pair % NX
                halves = []
                for i in range(2):
                    row = (p * 4 + z + i) * NX + x_at
                    halves.append(accr[pl.ds(pl.multiple_of(row * 16 + side * 8, 8), 8), :])
                both = jnp.concatenate(halves, 0)
                for y in range(NY):
                    slot = (y, x_at)
                    table[slot + (slice(128 + z * 8, 144 + z * 8),)] = both[:, y * 128 : y * 128 + 128]


def layer(where, x, pasts, keep, cot, conv, res, theirs):
    rows = [((ROWS, WIDTH), BF16), ((ROWS, WIDTH), F32), ((ROWS - FIRST, WIDTH), BF16)]
    totals = [(BIG, F32), (BIG, F32), (SMALL, F32)]
    aliases = {6 + j: j for j in range(6)}
    ins = lambda i: [x, pasts[i], keep, cot, conv, res]
    kernel = lambda f, i: functools.partial(f, PARTS[i])
    x_far, cot_far = x, cot
    carry = dict(aliases=aliases, **LAYER)
    count = PARTS[0][1]
    state = call(
        kernel(first_kernel, 0),
        "layer_first",
        [x_far, pasts[0], keep, cot_far, conv, res],
        rows + totals,
        far=(0, 3, 5),
        loose=(1,),
        scratch=[pltpu.VMEM((count, WIDTH), BF16)] * 3 + [pltpu.VMEM((WIDTH, WIDTH), BF16), pltpu.SemaphoreType.DMA((16,))],
        **LAYER,
    )
    *done, s0, s1, s2 = call(kernel(next_kernel, 1), "layer_next", [*ins(1), *state], rows + totals, **carry)
    *sums, later = call(
        later_kernel,
        "layer_later",
        [x, theirs, conv, res, s0, s1, s2],
        [*totals, ((FIRST, WIDTH), BF16)],
        aliases={4: 0, 5: 1, 6: 2},
        **LAYER,
    )
    out, cur, prior, _, _, _, own0, own1, send0, send1 = call(
        kernel(last_kernel, 2),
        "layer_last",
        [*ins(2), *done, *sums],
        [*rows, *totals, *[(TABLE, F32)] * 4],
        where,
        **carry,
    )
    return out, cur, prior, later, (own0, own1), (send0, send1)


def after_core(near, where, own, got, keep, send):
    y = where[1]
    for i, (stay, leave) in enumerate(((0, near), (4 - near, 2))):
        keep[i] = own[y ^ stay] + got[y ^ stay]
        send[i] = (own[y ^ leave] + got[y ^ leave]).astype(BF16)


def after_y(keep, got, own, send):
    own[...] = keep[0] + got[0].astype(F32)
    send[...] = (keep[1] + got[1].astype(F32)).astype(BF16)


def before_seq(own0, got0, own1, got1, *rest):
    blocks = rest[-1]
    for p, (own, got) in enumerate(((own0, got0), (own1, got1))):
        for x in range(NX):
            total = own[x] + got[x].astype(F32)
            for z in range(4):
                rows = (total[z * 16 : z * 16 + 16], total[64 + z * 16 : 80 + z * 16], total[128 + z * 8 : 136 + z * 8])
                blocks[(p * 4 + z) * NX + x] = jnp.concatenate(rows, 0).astype(BF16)


def after_seq(pieces, out):
    total = pieces[0].astype(F32)
    for i in range(1, NX * NZ):
        total = total + pieces[i].astype(F32)
    out[...] = total * (1.0 / 512.0)


def join(where, mine, got, both):
    both[where[0]] = mine[...]
    both[1 - where[0]] = got[...]


def assemble(where, *refs):
    conv, res, table = refs[4:]
    for j, ref in zip((0, 1, 3, 2), refs):
        table[j] = ref[...]
    for y in range(NY):
        pair = table[where[1] ^ y]
        lanes = slice(y * 128, y * 128 + 128)
        for c in range(NC):
            conv[0, c * 16 : c * 16 + 16, lanes] = pair[c, :16]
            conv[1, c * 16 : c * 16 + 16, lanes] = pair[c, 16:32]
            res[c * 8 : c * 8 + 8, lanes] = pair[c, 32:]


def reduce_terms(where, own, send, following, out):
    pair, half = (2,) + HALF, HALF
    got = [grp_swap(table, 1) for table in send]
    keep, own_y, got_y = [], [], []
    for p, near in enumerate((1, 3)):
        kernel = functools.partial(after_core, near)
        kept, leaving = call(kernel, "after_core", [own[p], got[p]], [(pair, F32), (pair, BF16)], where)
        keep.append(kept)
        got_y.append(y_swap(leaving, near))
    for p, far in enumerate((3, 1)):
        mine, leaving = call(after_y, "after_y", [keep[p], got_y[p]], [(half, F32), (half, BF16)])
        own_y += [mine, y_swap(leaving, far)]
    (blocks,) = call(before_seq, "before_seq", [*own_y, following, out], [((NX * NZ,) + PIECE, BF16)], far=(5,))
    pieces = lax.all_to_all(blocks, "seq", 0, 0)
    (mine,) = call(after_seq, "after_seq", [pieces], [(PIECE, F32)])
    (both,) = call(join, "join", [mine, grp_swap(mine, 1)], [((2,) + PIECE, F32)], where)
    table = {0: both}
    for j in (2, 1, 3):
        table[j] = y_swap(both, j)
    conv, res = call(
        assemble,
        "assemble",
        [table[j] for j in (0, 1, 3, 2)],
        [((2, 32, WIDTH), F32), ((16, WIDTH), F32)],
        where,
        [pltpu.VMEM((4, 2) + PIECE, F32)],
        free_outs=True,
    )
    return conv.swapaxes(1, 2), res.T


def local(inputs, offsets, conv_weight, res_weight, cotangent):
    x, cot = inputs[0], cotangent[0]
    jump = DILATION_GAP // ROWS
    grp, seq = lax.axis_index("grp"), lax.axis_index("seq")
    where = jnp.stack([grp & 1, grp >> 1, seq & 3, seq >> 2]).astype(jnp.int32)
    keep = jnp.broadcast_to((offsets[0] >= DILATION_GAP).astype(BF16)[:, None], (ROWS, 128))
    chunks, mine = split_all(keep, x, cot)
    pasts = [shifted(chunk, jump) for chunk in chunks]
    theirs = shifted(mine, -jump)
    out, cur, prior, later, own, send = layer(
        where, x, pasts, keep, cot, conv_weight, res_weight, theirs
    )
    following = shifted(prior, -jump)
    past_first = shifted(x[:FIRST], jump)
    out, cur = call(
        own_first_kernel,
        "layer_own_first",
        [x, past_first, keep, cot, conv_weight, res_weight, out, cur],
        [((ROWS, WIDTH), BF16), ((ROWS, WIDTH), F32)],
        aliases={6: 0, 7: 1},
        **LAYER,
    )
    (out,) = call(flush, "flush", [out], [((ROWS, WIDTH), BF16)], scratch=[pltpu.SemaphoreType.DMA((1,))], far_outs=True)
    d_conv, d_res = reduce_terms(where, own, send, following, out)
    d_inputs = (cur + jnp.concatenate([later, following], 0).astype(F32)).astype(BF16)
    return (out[None], d_inputs[None], d_conv, d_res)


def solution(mesh):
    placed = (P("grp", "seq", None), P("grp", "seq"), P(), P(), P("grp", "seq", None))
    return jax.shard_map(
        local,
        mesh=mesh,
        in_specs=placed,
        out_specs=(
            P("grp", "seq", None),
            P("grp", "seq", None),
            P(None, None, "seq"),
            P(None, "seq"),
        ),
        check_vma=False,
    )
```
